32 devices in a mesh: fsdp: 4 (over z), ctx: 4 (over y, core), tp: 2 (over x).
Axes of the slice: x: 2, y: 2, z: 4, core: 2. Of those that a mesh axis runs over, the one named last changes fastest.
Arguments:
- block_input: bfloat16 [4, 1024, 1024], P('fsdp', 'ctx'), may hold values from -6 to 6
- input_gain: float32 [1024], replicated, may hold values from 0.5 to 1.5
- gate_proj: bfloat16 [1024, 2048], P('fsdp', 'tp'), may hold values from -0.1875 to 0.1875
- x_proj: bfloat16 [1024, 2048], P('fsdp', 'tp'), may hold values from -0.1875 to 0.1875
- bc_proj: bfloat16 [1024, 256], P('fsdp'), may hold values from -0.1875 to 0.1875
- dt_proj: bfloat16 [1024, 32], P('fsdp', 'tp'), may hold values from -0.1875 to 0.1875
- x_conv: float32 [4, 2048], P(None, 'tp'), may hold values from -3 to 3
- bc_conv: float32 [4, 256], replicated, may hold values from -3 to 3
- dt_bias: float32 [32], P('tp'), may hold values from -2 to 1
- a_log: float32 [32], P('tp'), may hold values from -11 to -2
- skip_gain: float32 [32], P('tp'), may hold values from 0.5 to 1.5
- gated_gain: float32 [2048], P('tp'), may hold values from 0.5 to 1.5
- out_proj: bfloat16 [2048, 1024], P('tp', 'fsdp'), may hold values from -0.125 to 0.125
- cotangent: bfloat16 [4, 1024, 1024], P('fsdp', 'ctx'), may hold values from -6 to 6
Outputs:
- block_output: bfloat16 [4, 1024, 1024], P('fsdp', 'ctx')
- input_grad: float32 [4, 1024, 1024], P('fsdp', 'ctx')
- grad_input_gain: float32 [1024], replicated
- grad_gate_proj: float32 [1024, 2048], P('fsdp', 'tp')
- grad_x_proj: float32 [1024, 2048], P('fsdp', 'tp')
- grad_bc_proj: float32 [1024, 256], P('fsdp')
- grad_dt_proj: float32 [1024, 32], P('fsdp', 'tp')
- grad_x_conv: float32 [4, 2048], P(None, 'tp')
- grad_bc_conv: float32 [4, 256], replicated
- grad_dt_bias: float32 [32], P('tp')
- grad_a_log: float32 [32], P('tp')
- grad_skip_gain: float32 [32], P('tp')
- grad_gated_gain: float32 [2048], P('tp')
- grad_out_proj: float32 [2048, 1024], P('tp', 'fsdp')
The draws below stay inside these ranges and needn't reach their ends.
All inputs are finite; a program needn't handle non-finite values.
Results may differ from the reference program's by a relative error of at most 0.0098.
Values may be sent and summed in bfloat16 or wider, within the bound.
No kernel may reach another device: no remote copies, remote signals or barrier semaphores. Data moves between devices by JAX's collectives and lax.ppermute only.
A program may use at most 128 MiB of HBM per device.

```python
import jax
import jax.numpy as jnp
from jax import lax

D = 1024
HEADDIM = 64
NSTATE = 128
INNER = 2048
NHEADS = 32
KCONV = 4
GROUP = 256
SEQLEN = 1024
BATCH = 4


def block_scale(key, shape, cuts, smallest, largest):
    def one(dim, parts):
        steps = jax.random.uniform(jax.random.fold_in(jax.random.fold_in(key, 6), dim), (parts,), jnp.float32, smallest / len(cuts), largest / len(cuts))
        return jnp.repeat(jnp.exp(steps), shape[dim] // parts).reshape((-1,) + (1,) * (len(shape) - dim - 1))

    factor_of = one(*cuts[0])
    for cut in cuts[1:]:
        factor_of = factor_of * one(*cut)
    return factor_of


def gaussian(key, shape, deviation, most, split=(), kind=jnp.bfloat16):
    factor_of = block_scale(key, shape, split, -0.22, 0.18) if split else 1.0
    values = jax.random.normal(key, shape, jnp.float32) * deviation * factor_of
    return jnp.minimum(jnp.maximum(values, -most), most).astype(kind)


def setup_inputs(seed: int = 0) -> dict:
    seeds = jax.random.split(jax.random.key(seed), 15)
    return {
        "block_input": gaussian(seeds[0], (BATCH, SEQLEN, D), 1.0, 6.0, ((0, 4), (1, 4))),
        "input_gain": jnp.clip(1.0 + 0.1 * jax.random.normal(seeds[1], (D,), jnp.float32), 0.5, 1.5),
        "gate_proj": gaussian(seeds[2], (D, INNER), D ** -0.5, 0.1875, ((0, 4), (1, 2))),
        "x_proj": gaussian(seeds[3], (D, INNER), D ** -0.5, 0.1875, ((0, 4), (1, 2))),
        "bc_proj": gaussian(seeds[4], (D, 2 * NSTATE), D ** -0.5, 0.1875, ((0, 4),)),
        "dt_proj": gaussian(seeds[5], (D, NHEADS), D ** -0.5, 0.1875, ((0, 4), (1, 2))),
        "x_conv": gaussian(seeds[6], (KCONV, INNER), KCONV ** -0.5, 3.0, ((1, 2),), jnp.float32),
        "bc_conv": gaussian(seeds[7], (KCONV, 2 * NSTATE), KCONV ** -0.5, 3.0, (), jnp.float32),
        "dt_bias": jnp.clip(-2.0 + 3.0 * jax.random.uniform(seeds[8], (NHEADS,), jnp.float32) ** block_scale(seeds[8], (NHEADS,), ((0, 2),), -0.2, 0.2), -2.0, 1.0),
        "a_log": jnp.clip(-11.0 + 9.0 * jax.random.uniform(seeds[9], (NHEADS,), jnp.float32) ** block_scale(seeds[9], (NHEADS,), ((0, 2),), -0.2, 0.2), -11.0, -2.0),
        "skip_gain": jnp.clip(0.5 + 1.0 * jax.random.uniform(seeds[10], (NHEADS,), jnp.float32) ** block_scale(seeds[10], (NHEADS,), ((0, 2),), -0.2, 0.2), 0.5, 1.5),
        "gated_gain": jnp.clip(1.0 + 0.1 * jax.random.normal(seeds[11], (INNER,), jnp.float32), 0.5, 1.5),
        "out_proj": gaussian(seeds[12], (INNER, D), INNER ** -0.5, 0.125, ((0, 2), (1, 4))),
        "cotangent": gaussian(seeds[13], (BATCH, SEQLEN, D), 1.0, 6.0, ((0, 4), (1, 4))),
    }


EPSILON = 1e-05
FINE = lax.Precision.HIGHEST

@jax.custom_vjp
def low(v):
    return lax.optimization_barrier(v.astype(jnp.bfloat16)).astype(jnp.float32)

@jax.custom_vjp
def low_back(v):
    return v

def low_keep(v):
    return (low(v), None)

def low_pass(kept, grad):
    return (grad,)

def back_keep(v):
    return (v, None)

def back_low(kept, grad):
    return (low(grad),)
low.defvjp(low_keep, low_pass)
low_back.defvjp(back_keep, back_low)

def matmul(left, right):
    return jnp.dot(left, right, precision=FINE, preferred_element_type=jnp.float32)

def causal_conv(values, kernel_taps):
    tap_count = kernel_taps.shape[0]
    padded = jnp.concatenate([jnp.zeros((tap_count - 1, values.shape[1]), jnp.float32), values], axis=0)
    total = jnp.zeros_like(values)
    for offset in range(tap_count):
        total = total + kernel_taps[offset] * padded[offset:offset + values.shape[0]]
    return total

def block_step(state_in, pieces):
    x_part, b_part, c_part, step_part, decay_part = pieces
    cumulative = jnp.cumsum(decay_part, axis=0)
    log_gaps = cumulative[:, None, :] - cumulative[None, :, :]
    causal = jnp.tril(jnp.ones((GROUP, GROUP), jnp.bool_))[:, :, None]
    decays = jnp.where(causal, jnp.exp(jnp.where(causal, log_gaps, 0.0)), 0.0)
    scores = matmul(c_part, b_part.T)
    weights = decays * scores[:, :, None] * step_part[None, :, :]
    within = jnp.einsum('tsh,shp->thp', weights, x_part, precision=FINE)
    carried = jnp.exp(cumulative)[:, :, None] * jnp.einsum('tn,hpn->thp', c_part, state_in, precision=FINE)
    tail_decay = jnp.exp(cumulative[-1][None, :] - cumulative) * step_part
    state_out = jnp.exp(cumulative[-1])[:, None, None] * state_in + jnp.einsum('sh,shp,sn->hpn', tail_decay, x_part, b_part, precision=FINE)
    return (state_out, within + carried)

def mamba_block(residual, input_gain, gate_proj, x_proj, bc_proj, dt_proj, x_conv, bc_conv, dt_bias, a_log, skip_gain, gated_gain, out_proj):
    in_scale = lax.rsqrt(lax.optimization_barrier(jnp.mean(residual * residual, axis=-1, keepdims=True)) + EPSILON)
    normed = low(residual * in_scale * input_gain)
    gate_input = low_back(matmul(normed, gate_proj))
    x_input = low_back(matmul(normed, x_proj))
    bc_input = low_back(matmul(normed, bc_proj))
    dt_input = low_back(matmul(normed, dt_proj))
    x_act = jax.nn.silu(causal_conv(x_input, x_conv))
    bc_act = jax.nn.silu(causal_conv(bc_input, bc_conv))
    step_size = jax.nn.softplus(dt_input + dt_bias)
    log_decay = -jnp.exp(a_log) * step_size
    x_heads = x_act.reshape(SEQLEN, NHEADS, HEADDIM)
    block_count = SEQLEN // GROUP
    pieces = (x_heads.reshape(block_count, GROUP, NHEADS, HEADDIM), bc_act[:, :NSTATE].reshape(block_count, GROUP, NSTATE), bc_act[:, NSTATE:].reshape(block_count, GROUP, NSTATE), step_size.reshape(block_count, GROUP, NHEADS), log_decay.reshape(block_count, GROUP, NHEADS))
    initial = jnp.zeros((NHEADS, HEADDIM, NSTATE), jnp.float32)
    final_state, mixed_blocks = lax.scan(jax.checkpoint(block_step), initial, pieces)
    mixed_heads = mixed_blocks.reshape(SEQLEN, NHEADS, HEADDIM) + skip_gain[:, None] * x_heads
    gated_rows = mixed_heads.reshape(SEQLEN, INNER) * jax.nn.silu(gate_input)
    out_scale = lax.rsqrt(lax.optimization_barrier(jnp.mean(gated_rows * gated_rows, axis=-1, keepdims=True)) + EPSILON)
    normed_out = low_back(low(gated_rows * out_scale * gated_gain))
    return residual + matmul(normed_out, out_proj)

def reference(block_input, input_gain, gate_proj, x_proj, bc_proj, dt_proj, x_conv, bc_conv, dt_bias, a_log, skip_gain, gated_gain, out_proj, cotangent):
    parameters = tuple((item.astype(jnp.float32) for item in (input_gain, gate_proj, x_proj, bc_proj, dt_proj, x_conv, bc_conv, dt_bias, a_log, skip_gain, gated_gain, out_proj)))

    def one_sequence(totals, seq_pair):
        sequence, sequence_cot = seq_pair
        result, pullback = jax.vjp(mamba_block, sequence.astype(jnp.float32), *parameters)
        gradients = pullback(sequence_cot.astype(jnp.float32))
        totals = tuple((total + grad_part for total, grad_part in zip(totals, gradients[1:])))
        return (totals, (result.astype(jnp.bfloat16), gradients[0]))
    zero_totals = tuple((jnp.zeros_like(item) for item in parameters))
    totals, (results, input_grads) = lax.scan(one_sequence, zero_totals, (block_input, cotangent))
    return (results, input_grads, totals[0], totals[1], totals[2], totals[3], totals[4], totals[5], totals[6], totals[7], totals[8], totals[9], totals[10], totals[11])
```

```python
import jax
import jax.numpy as jnp
from jax import lax
from jax.experimental import pallas as pl
from jax.experimental.pallas import tpu as pltpu
from jax.sharding import PartitionSpec as P

EPSILON = 1e-05
FINE = lax.Precision.HIGHEST
F32 = jnp.float32
LOW = jnp.bfloat16
HALO = 16
LANES = 128
NEVER = -1e30


def swap(block, axis, bits):
    count = lax.axis_size(axis)
    return lax.ppermute(block, axis, [(i, i ^ bits) for i in range(count)])


def bits_of(axis):
    return [1 << b for b in range(lax.axis_size(axis).bit_length() - 1)]


def spread(block, axis):
    pieces = {0: block}
    for bit in reversed(bits_of(axis)):
        pieces.update({k ^ bit: swap(v, axis, bit) for k, v in list(pieces.items())})
    return [pieces[k] for k in range(len(pieces))]


def after(value, *earlier):
    return lax.optimization_barrier((value, *earlier))[0]


def launch(body, outs, place, *args, scratch=(), mib=40, flops=0):
    moved = sum(a.size * a.dtype.itemsize for a in args)
    return pl.pallas_call(
        body,
        out_shape=[jax.ShapeDtypeStruct(s, d) for s, d in outs],
        in_specs=[pl.BlockSpec(memory_space=pltpu.SMEM)]
        + [pl.BlockSpec(memory_space=pltpu.VMEM)] * len(args),
        out_specs=[pl.BlockSpec(memory_space=pltpu.VMEM)] * len(outs),
        scratch_shapes=[pltpu.VMEM(s, d) for s, d in scratch],
        compiler_params=pltpu.CompilerParams(vmem_limit_bytes=mib << 20),
        cost_estimate=pl.CostEstimate(flops=flops, bytes_accessed=moved, transcendentals=0),
    )(place, *args)


def aligned(start, count):
    return pl.ds(pl.multiple_of(start, count), count)


def mm(a, b, dims=((1,), (0,))):
    return lax.dot_general(
        a.astype(LOW), b.astype(LOW), (dims, ((), ())), preferred_element_type=F32
    )


NT = ((1,), (1,))
TN = ((0,), (0,))


def fine(a, b):
    return lax.dot_general(
        a, b, (((1,), (0,)), ((), ())), precision=FINE, preferred_element_type=F32
    )


def split_mm(a, b):
    high = a.astype(LOW)
    return mm(high, b) + mm(a - high.astype(F32), b)


def sigmoid(v):
    return 1.0 / (1.0 + jnp.exp(-v))


def silu_slope(v, s):
    return s * (1.0 + v * (1.0 - s))


def iota(shape, dim):
    return lax.broadcasted_iota(jnp.int32, shape, dim)


def pair_wide(v, i, per):
    rows = v.shape[0]
    first = iota((rows, LANES), 1) < LANES // per
    return jnp.where(first, v[:, per * i : per * i + 1], v[:, per * i + 1 : per * i + 2])


def head_of_unit(units, size):
    return iota((units, LANES), 0) // size == iota((units, LANES), 1)


def as_column(row, units, size):
    return jnp.sum(jnp.where(head_of_unit(units, size), row[0:1], 0.0), axis=1, keepdims=True)


def pack_body(place, rows, xp, bcp, dtp, gp, op, first, gate_q, out_q, halo, dt_wide):
    part, inner = gate_q.shape
    here = aligned(place[1] * part, part)
    heads = dtp.shape[1]
    blank = jnp.zeros((dtp.shape[0], LANES - heads), LOW)
    dt_wide[...] = jnp.concatenate([dtp[...], blank], axis=1)
    states = bcp.shape[1]
    first[:, :inner] = xp[here, :]
    first[:, inner : inner + states] = bcp[here, :]
    first[:, inner + states :] = dt_wide[here, :]
    gate_q[...] = gp[here, :]
    out_q[...] = op[aligned(place[1] * out_q.shape[0], out_q.shape[0]), :]
    halo[...] = rows[rows.shape[0] - HALO :, :]


def norm_rows(v, gain):
    v = v.astype(F32)
    return v * lax.rsqrt(jnp.mean(v * v, axis=-1, keepdims=True) + EPSILON) * gain


def norm_body(place, rows, halo, gain, normed):
    normed[:HALO] = norm_rows(halo[...], gain[...]).astype(LOW)
    for at in range(0, rows.shape[0], 64):
        normed[HALO + at : HALO + at + 64] = norm_rows(rows[at : at + 64], gain[...]).astype(LOW)


def front_body(fsdp, ctx, taps, heads, size):
    def body(place, normed, xp, bcp, dtp, *rest):
        parts = rest[:ctx]
        x_conv, bc_conv, dt_bias, a_log = rest[ctx : ctx + 4]
        w_all, proj, conv_out, act, within, state, scalars, w_x = rest[ctx + 4 :]
        z, c = place[0], place[1]
        shard, inner = xp.shape
        both = inner + bcp.shape[1]
        half_bc = bcp.shape[1] // 2
        own = aligned(z * shard, shard)
        w_all[own, :inner] = xp[...]
        w_all[own, inner:both] = bcp[...]
        w_all[own, both:] = dtp[...]
        n = shard // ctx
        for j in range(ctx):
            for k in range(1, fsdp):
                w_all[aligned((z ^ k) * shard + (c ^ j) * n, n), :] = parts[j][k - 1]
        proj[...] = jnp.dot(normed[...], w_all[...], preferred_element_type=F32)
        length = conv_out.shape[0]
        start = HALO - taps + 1
        for at in range(0, both, LANES):
            cols = slice(at, at + LANES)
            if at < inner:
                tap = x_conv[:, cols]
            else:
                tap = bc_conv[:, at - inner : at - inner + LANES]
            total = tap[0:1] * proj[start : start + length, cols]
            for k in range(1, taps):
                total = total + tap[k : k + 1] * proj[start + k : start + k + length, cols]
            conv_out[:, cols] = total
            act[:, cols] = total * sigmoid(total)
        pre = proj[HALO:, both:] + dt_bias[...]
        step = jnp.maximum(pre, 0.0) + jnp.log1p(jnp.exp(-jnp.abs(pre)))
        log_decay = -jnp.exp(a_log[...]) * step
        lower = iota((length, length), 0) >= iota((length, length), 1)
        cum = fine(jnp.where(lower, 1.0, 0.0), log_decay)
        cum_t = cum.T
        scalars[0] = step
        scalars[1] = cum
        scalars[2] = jnp.exp(cum)
        tail = jnp.exp(cum[length - 1 :] - cum)
        scalars[3] = tail
        b_low = act[:, inner : inner + half_bc].astype(LOW)
        c_low = act[:, inner + half_bc :].astype(LOW)
        scores = mm(c_low, b_low, NT)
        half = length // 2
        per = LANES // size
        first = iota((half, LANES), 1) < size
        for i in range(heads // per):
            cols = slice(LANES * i, LANES * i + LANES)
            stepped = act[:, cols] * pair_wide(step, i, per)
            w_x[:, cols] = (stepped * pair_wide(tail, i, per)).astype(LOW)
            low = stepped.astype(LOW)
            tops, bottoms = [], []
            for h in range(per * i, per * i + per):
                gaps = cum[:half, h : h + 1] - cum_t[h : h + 1, :half]
                top = jnp.exp(jnp.where(lower[:half, :half], gaps, NEVER)) * scores[:half, :half]
                gaps = cum[half:, h : h + 1] - cum_t[h : h + 1, :]
                bottom = jnp.exp(jnp.where(lower[half:], gaps, NEVER)) * scores[half:]
                tops.append(mm(top, low[:half]))
                bottoms.append(mm(bottom, low))
            within[:half, cols] = jnp.where(first, tops[0], tops[1])
            within[half:, cols] = jnp.where(first, bottoms[0], bottoms[1])
        state[...] = mm(w_x[...], b_low, TN).astype(LOW)

    return body


def merge(before, keep, other, decay, other_decay, size):
    units = keep.shape[0]
    earlier = other * as_column(decay, units, size) + keep
    later = keep * as_column(other_decay, units, size) + other
    return jnp.where(before, earlier, later)


def scan_body(bit, reverse, size, first):
    def body(place, state, other, decay, other_decay, *rest):
        if first:
            total, total_decay, prefix, prefix_decay = rest
        else:
            old, old_decay, total, total_decay, prefix, prefix_decay = rest
        before = ((place[1] & bit) != 0) != reverse
        mine, theirs = state[...].astype(F32), other[...].astype(F32)
        total[...] = merge(before, mine, theirs, decay[...], other_decay[...], size).astype(LOW)
        total_decay[...] = decay[...] * other_decay[...]
        if first:
            prefix[...] = jnp.where(before, theirs, 0.0).astype(LOW)
            prefix_decay[...] = jnp.where(before, other_decay[...], 1.0)
        else:
            units = state.shape[0]
            kept = old[...].astype(F32)
            grown = theirs * as_column(old_decay[...], units, size) + kept
            prefix[...] = jnp.where(before, grown, kept).astype(LOW)
            prefix_decay[...] = jnp.where(before, old_decay[...] * other_decay[...], old_decay[...])

    return body


def run_scan(place, state, decay, reverse, size):
    bits = bits_of("ctx")
    kept = ()
    for bit in bits[:-1]:
        other, other_decay = swap(state, "ctx", bit), swap(decay, "ctx", bit)
        outs = [(state.shape, LOW), (decay.shape, F32)] * 2
        state, decay, *kept = launch(
            scan_body(bit, reverse, size, not kept),
            outs,
            place,
            state,
            other,
            decay,
            other_decay,
            *kept,
            mib=16,
        )
    return swap(state, "ctx", bits[-1]), kept[0], kept[1]


def last_prefix(before, other, kept, kept_decay, size):
    kept_f = kept[...].astype(F32)
    grown = other[...].astype(F32) * as_column(kept_decay[0:1], kept.shape[0], size) + kept_f
    return jnp.where(before, grown, kept_f)


def gate_body(fsdp, ctx):
    def body(place, normed, cot, gp, op, *rest):
        g_parts, o_parts = rest[:ctx], rest[ctx : 2 * ctx]
        gate_in, d_normed_out, w_gate, w_out = rest[2 * ctx :]
        z, c = place[0], place[1]
        shard = gp.shape[0]
        w_gate[aligned(z * shard, shard), :] = gp[...]
        span = op.shape[1]
        w_out[:, aligned(z * span, span)] = op[...]
        n, m = shard // ctx, op.shape[0] // ctx
        for j in range(ctx):
            for k in range(1, fsdp):
                w_gate[aligned((z ^ k) * shard + (c ^ j) * n, n), :] = g_parts[j][k - 1]
                w_out[aligned((c ^ j) * m, m), aligned((z ^ k) * span, span)] = o_parts[j][k - 1]
        gate_in[...] = jnp.dot(normed[HALO:], w_gate[...], preferred_element_type=F32)
        d_normed_out[...] = mm(cot[...], w_out[...], NT).astype(LOW)

    return body


def mix_body(bit, size):
    def body(
        place, other, kept, kept_decay, act, within, scalars, gate_in, d_no, skip, gain,
        state_in, swept, sums,
    ):
        before = (place[1] & bit) != 0
        state_in[...] = last_prefix(before, other, kept, kept_decay, size).astype(LOW)
        length, inner = within.shape
        half_bc = (act.shape[1] - inner) // 2
        c_low = act[:, inner + half_bc :].astype(LOW)
        grow = scalars[2]
        per = LANES // size
        squares = jnp.zeros((length, LANES), F32)
        crosses = jnp.zeros((length, LANES), F32)
        for i in range(inner // LANES):
            cols = slice(LANES * i, LANES * i + LANES)
            carried = mm(c_low, state_in[cols, :], NT)
            flow = within[:, cols] + pair_wide(grow, i, per) * carried
            swept[:, cols] = flow
            mixed = flow + skip[:, cols] * act[:, cols]
            gate = gate_in[:, cols]
            gated = mixed * gate * sigmoid(gate)
            squares = squares + gated * gated
            crosses = crosses + d_no[:, cols].astype(F32) * gain[:, cols] * gated
        lane = iota((length, LANES), 1)
        pair = jnp.where(
            lane == 0,
            jnp.sum(squares, axis=1, keepdims=True),
            jnp.where(lane == 1, jnp.sum(crosses, axis=1, keepdims=True), 0.0),
        )
        sums[...] = pair.T[:8]

    return body


def turn_body(size, full_inner):
    def body(
        place, mine, theirs, act, swept, scalars, gate_in, d_no, skip, gain,
        normed_out, d_gate, d_mixed, d_scaled, state_grad, rows_out,
    ):
        length, inner = swept.shape
        half_bc = (act.shape[1] - inner) // 2
        both = (mine[...] + theirs[...]).T
        scale = lax.rsqrt(both[:, 0:1] / full_inner + EPSILON)
        cross = scale * scale * scale / full_inner * both[:, 1:2]
        grow = scalars[2]
        per = LANES // size
        rows_out[...] = jnp.zeros(rows_out.shape, F32)
        for i in range(inner // LANES):
            cols = slice(LANES * i, LANES * i + LANES)
            x_act = act[:, cols]
            mixed = swept[:, cols] + skip[:, cols] * x_act
            gate = gate_in[:, cols]
            s = sigmoid(gate)
            gated = mixed * gate * s
            grad = d_no[:, cols].astype(F32)
            scaled = gated * scale
            normed_out[:, cols] = (scaled * gain[:, cols]).astype(LOW)
            rows_out[0:1, cols] = jnp.sum(grad * scaled, axis=0, keepdims=True)
            d_gated = scale * gain[:, cols] * grad - gated * cross
            d_gate[:, cols] = (d_gated * mixed * silu_slope(gate, s)).astype(LOW)
            dm = d_gated * gate * s
            d_mixed[:, cols] = dm
            rows_out[1:2, cols] = jnp.sum(dm * x_act, axis=0, keepdims=True)
            d_scaled[:, cols] = (dm * pair_wide(grow, i, per)).astype(LOW)
        c_low = act[:, inner + half_bc :].astype(LOW)
        state_grad[...] = mm(d_scaled[...], c_low, TN).astype(LOW)

    return body


def deal_body(ctx):
    def body(place, d_gate, normed_out, *rest):
        sends, stage = rest[:ctx], rest[ctx]
        w = sends[0].shape[2]
        for q in range(ctx):
            stage[q, 0] = d_gate[:, q * w : q * w + w]
            stage[q, 1] = normed_out[:, q * w : q * w + w]
        for k in range(ctx):
            sends[k][...] = stage[place[1] ^ k]

    return body


def local_body(heads, size):
    def body(place, d_mixed, act, scalars, rows, normed_out, w_out, back, pair_t, half_out, branch):
        length, inner = d_mixed.shape
        half_bc = (act.shape[1] - inner) // 2
        out = jnp.dot(normed_out[...], w_out[...], preferred_element_type=F32)
        branch[...] = out.astype(LOW)
        half_out[...] = rows[...].astype(F32) + out
        step, cum = scalars[0], scalars[1]
        cum_t = cum.T
        upper = iota((length, length), 0) <= iota((length, length), 1)
        b_low = act[:, inner : inner + half_bc].astype(LOW)
        c_low = act[:, inner + half_bc :].astype(LOW)
        scores = mm(b_low, c_low, NT)
        half = length // 2
        per = LANES // size
        first = iota((length, LANES), 1) < size
        pair_t[...] = jnp.zeros(pair_t.shape, F32)
        for i in range(heads // per):
            cols = slice(LANES * i, LANES * i + LANES)
            stepped = act[:, cols] * pair_wide(step, i, per)
            grad = d_mixed[:, cols].astype(LOW)
            tops, bottoms = [], []
            for h in range(per * i, per * i + per):
                mask = first if h == per * i else jnp.logical_not(first)
                mine = jnp.where(mask, stepped, 0.0).astype(LOW)
                gaps = cum_t[h : h + 1, :] - cum[:half, h : h + 1]
                top = jnp.exp(jnp.where(upper[:half], gaps, NEVER))
                gaps = cum_t[h : h + 1, half:] - cum[half:, h : h + 1]
                bottom = jnp.exp(jnp.where(upper[half:, half:], gaps, NEVER))
                pair_t[:half] += top * mm(mine[:half], grad, NT)
                pair_t[half:, half:] += bottom * mm(mine[half:], grad[half:], NT)
                tops.append(mm(top * scores[:half], grad))
                bottoms.append(mm(bottom * scores[half:, half:], grad[half:]))
            back[:half, cols] = jnp.where(first[:half], tops[0], tops[1])
            back[half:, cols] = jnp.where(first[:half], bottoms[0], bottoms[1])

    return body


def rear_body(bit, ctx, taps, heads, size):
    def body(
        place, other, kept, kept_decay, back, pair_t, act, conv_out, proj, scalars, swept, d_mixed,
        d_scaled, state_in, skip, skip_rows, x_conv, bc_conv, dt_bias, a_log, *rest,
    ):
        d_first, small = rest[:2]
        sends = rest[2 : 2 + ctx]
        spaced, tails, dots, sweeps, stage = rest[2 + ctx :]
        length, inner = back.shape
        both = act.shape[1]
        half_bc = (both - inner) // 2
        before = (place[1] & bit) == 0
        later_f = last_prefix(before, other, kept, kept_decay, size)
        later = later_f.astype(LOW)
        step, cum, tail = scalars[0], scalars[1], scalars[3]
        b_low = act[:, inner : inner + half_bc].astype(LOW)
        c_low = act[:, inner + half_bc :].astype(LOW)
        per = LANES // size
        ones_at = jnp.where(head_of_unit(inner, size), 1.0, 0.0)
        small[...] = jnp.zeros(small.shape, F32)
        spaced[:HALO] = jnp.zeros((HALO, both), F32)
        spaced[HALO + length :] = jnp.zeros((HALO, both), F32)
        last_rows = []
        for i in range(inner // LANES):
            cols = slice(LANES * i, LANES * i + LANES)
            x_act = act[:, cols]
            wide_step = pair_wide(step, i, per)
            stepped = x_act * wide_step
            wide_tail = pair_wide(tail, i, per)
            tails[:, cols] = (stepped * wide_tail).astype(LOW)
            extra = wide_tail * mm(b_low, later[cols, :], NT)
            last_rows.append(jnp.sum(stepped * extra, axis=0, keepdims=True))
            whole = back[:, cols] + extra
            grad = d_mixed[:, cols]
            dots[:, cols] = x_act * whole
            sweeps[:, cols] = grad * swept[:, cols]
            v = conv_out[:, cols]
            spaced[HALO : HALO + length, cols] = (
                wide_step * whole + skip[:, cols] * grad
            ) * silu_slope(v, sigmoid(v))
        pair = pair_t[...]
        d_b = mm(pair, c_low) + mm(tails[...], later)
        d_c = mm(pair, b_low, TN) + mm(d_scaled[...], state_in[...])
        for at, d in ((inner, d_b), (inner + half_bc, d_c)):
            v = conv_out[:, at : at + half_bc]
            spaced[HALO : HALO + length, at : at + half_bc] = d * silu_slope(v, sigmoid(v))
        start = HALO - taps + 1
        for at in range(0, both, LANES):
            cols = slice(at, at + LANES)
            if at < inner:
                tap = x_conv[:, cols]
            else:
                tap = bc_conv[:, at - inner : at - inner + LANES]
            grad = spaced[HALO : HALO + length, cols]
            total = tap[0:1] * spaced[taps - 1 : taps - 1 + HALO + length, cols]
            for k in range(1, taps):
                lead = taps - 1 - k
                total = total + tap[k : k + 1] * spaced[lead : lead + HALO + length, cols]
            d_first[:, cols] = total.astype(LOW)
            for k in range(taps):
                found = jnp.sum(
                    grad * proj[start + k : start + k + length, cols], axis=0, keepdims=True
                )
                if at < inner:
                    small[2 + k : 3 + k, cols] = found
                else:
                    put = k * (both - inner) + at - inner
                    small[1:2, put : put + LANES] = found
        d_step = split_mm(dots[...], ones_at)
        row_sum = split_mm(sweeps[...], ones_at)
        cross = jnp.sum(later_f * state_in[...].astype(F32), axis=1, keepdims=True)
        decay_grad = jnp.sum(jnp.where(ones_at > 0, cross, 0.0), axis=0, keepdims=True)
        tail_row = split_mm(
            jnp.broadcast_to(jnp.concatenate(last_rows, axis=1), (8, inner)), ones_at
        )[0:1]
        ends = tail_row + jnp.exp(cum[length - 1 :]) * decay_grad
        upper = jnp.where(iota((length, length), 0) <= iota((length, length), 1), 1.0, 0.0)
        d_log = fine(upper, row_sum - step * d_step) + ends
        rates = jnp.exp(a_log[...])
        pre = proj[HALO:, both:] + dt_bias[...]
        d_pre = (d_step - rates * d_log) * sigmoid(pre)
        d_pre = jnp.where(iota(d_pre.shape, 1) < heads, d_pre, 0.0)
        d_first[:HALO, both:] = jnp.zeros((HALO, LANES), LOW)
        d_first[HALO:, both:] = d_pre.astype(LOW)
        w = inner // ctx
        blank = 2 * LANES - LANES
        rest_width = both - inner + LANES + blank
        r = rest_width // ctx
        narrow = jnp.concatenate(
            [d_first[:, inner:], jnp.zeros((HALO + length, blank), LOW)], axis=1
        )
        for q in range(ctx):
            stage[q, :, :w] = d_first[:, q * w : q * w + w]
            stage[q, :, w:] = narrow[:, q * r : q * r + r]
        for k in range(ctx):
            sends[k][...] = stage[place[1] ^ k]
        small[6:7] = skip_rows[0:1]
        small[7:8, :LANES] = jnp.sum(d_pre, axis=0, keepdims=True)
        small[7:8, LANES : 2 * LANES] = jnp.sum(
            d_log * (-rates * step), axis=0, keepdims=True
        )
        small[7:8, 2 * LANES : 3 * LANES] = split_mm(
            jnp.broadcast_to(skip_rows[1:2], (8, inner)), ones_at
        )[0:1]

    return body


def down_body(place, d_first, d_gate, w_first, w_gate, rows, halo, small, own, send, edge, tally):
    grad = mm(d_first[...], w_first[...], NT)
    body = grad[HALO:] + mm(d_gate[...], w_gate[...], NT)
    own[...] = body
    send[...] = body.astype(LOW)
    edge[...] = grad[:HALO].astype(LOW)
    tally[...] = small[...]
    total = jnp.sum(grad[:HALO] * norm_rows(halo[...], 1.0), axis=0, keepdims=True)
    for at in range(0, rows.shape[0], 64):
        total = total + jnp.sum(
            body[at : at + 64] * norm_rows(rows[at : at + 64], 1.0), axis=0, keepdims=True
        )
    tally[0:1] = total


def weights_body(fsdp, ctx, stacked):
    def body(place, *rest):
        pieces, normeds = rest[:ctx], rest[ctx : 2 * ctx]
        rest = rest[2 * ctx :]
        cots = rest[: ctx if stacked else 0]
        own, *sends, part = rest[len(cots) :]
        for j in range(2 if stacked else 1):
            total = None
            for k in range(ctx):
                if stacked:
                    big = cots[k][...] if j else normeds[k][HALO:]
                    term = mm(pieces[k][j], big, TN)
                else:
                    term = mm(pieces[k][...], normeds[k][...], TN)
                total = term if total is None else total + term
            part[j] = total
        span = own.shape[2]
        own[...] = part[:, :, aligned(place[0] * span, span)]
        for k in range(1, fsdp):
            sends[k - 1][...] = part[:, :, aligned((place[0] ^ k) * span, span)].astype(LOW)

    return body


def close_body(ctx, inner, states, heads):
    def body(place, *rest):
        pairs, firsts, peers = rest[:ctx], rest[ctx : 2 * ctx], rest[2 * ctx : 3 * ctx]
        grad_gate, grad_out, grad_x, grad_bc, grad_dt, g_stage, x_stage, r_stage = rest[3 * ctx :]
        c = place[1]
        w = pairs[0].shape[1]
        r = peers[0].shape[1]
        for k in range(ctx):
            q = c ^ k
            g_stage[q] = pairs[k][0].astype(F32)
            grad_out[aligned(q * w, w), :] = pairs[k][1].astype(F32)
            x_stage[q] = firsts[k][0, :w].astype(F32)
            mine = firsts[k][0, w:].astype(F32)
            r_stage[0, aligned(q * r, r), :] = mine
            r_stage[1, aligned(q * r, r), :] = mine + peers[k][0].astype(F32)
        for q in range(ctx):
            grad_gate[:, q * w : q * w + w] = g_stage[q].T
            grad_x[:, q * w : q * w + w] = x_stage[q].T
        grad_bc[...] = r_stage[1, :states].T
        grad_dt[...] = r_stage[0, states : states + LANES].T[:, :heads]

    return body


def finish_body(place, own, peer, edge, edge_peer, rows, cot, gain, out):
    length, width = rows.shape
    extra = edge[...].astype(F32) + edge_peer[...].astype(F32)
    for at in range(0, length, 64):
        v = rows[at : at + 64].astype(F32)
        grad = own[at : at + 64] + peer[at : at + 64].astype(F32)
        if at + 64 == length:
            grad = grad + jnp.concatenate([jnp.zeros((64 - HALO, width), F32), extra])
        scale = lax.rsqrt(jnp.mean(v * v, axis=-1, keepdims=True) + EPSILON)
        d = grad * gain[...]
        inner = jnp.sum(d * v, axis=-1, keepdims=True)
        out[at : at + 64] = (
            cot[at : at + 64].astype(F32)
            + scale * d
            - v * (scale * scale * scale / width * inner)
        )


def on_device(
    block_input,
    input_gain,
    gate_proj,
    x_proj,
    bc_proj,
    dt_proj,
    x_conv,
    bc_conv,
    dt_bias,
    a_log,
    skip_gain,
    gated_gain,
    out_proj,
    cotangent,
):
    length, width = block_input.shape[1:]
    shard, inner = gate_proj.shape
    heads = dt_proj.shape[1]
    size = inner // heads
    states = bc_proj.shape[1]
    half_bc = states // 2
    taps = x_conv.shape[0]
    both = inner + states
    full_inner = inner * lax.axis_size("tp")
    ctx, fsdp = lax.axis_size("ctx"), lax.axis_size("fsdp")
    place = jnp.stack([lax.axis_index(a) for a in ("fsdp", "ctx", "tp")]).astype(jnp.int32)
    rows, cot = block_input[0], cotangent[0]
    ext = HALO + length
    last_bit = bits_of("ctx")[-1]

    first_q, gate_q, out_q, edge_rows, dt_wide = launch(
        pack_body,
        [
            ((shard // ctx, both + LANES), LOW),
            ((shard // ctx, inner), LOW),
            ((inner // ctx, out_proj.shape[1]), LOW),
            ((HALO, width), LOW),
            ((shard, LANES), LOW),
        ],
        place,
        rows,
        x_proj,
        bc_proj,
        dt_proj,
        gate_proj,
        out_proj,
        mib=16,
    )
    halo = lax.ppermute(edge_rows, "ctx", [(i, i + 1) for i in range(ctx - 1)])
    gain = input_gain[None]
    [normed] = launch(norm_body, [((ext, width), LOW)], place, rows, halo, gain, mib=16)

    def across(block):
        return [swap(block, "fsdp", k) for k in range(1, fsdp)]

    first_far = jnp.stack(across(first_q))
    first_parts = spread(first_far, "ctx")
    gate_q, out_q = after((gate_q, out_q), first_far)
    gate_far, out_far = jnp.stack(across(gate_q)), jnp.stack(across(out_q))
    gate_far, out_far = after((gate_far, out_far), first_parts[1])
    gate_parts, out_parts = spread(gate_far, "ctx"), spread(out_far, "ctx")
    late = after((normed, cot), gate_parts[-1])
    normed_all = [normed] + spread(late[0], "ctx")[1:]
    cot_all = [cot] + spread(late[1], "ctx")[1:]

    pad_heads = ((0, 0), (0, LANES - heads))
    bias_row = jnp.pad(dt_bias[None], pad_heads)
    a_row = jnp.pad(a_log[None], pad_heads)
    skip_row = jnp.repeat(skip_gain, size)[None]
    gained = gated_gain[None]
    w_first, proj, conv_out, act, within, state, scalars = launch(
        front_body(fsdp, ctx, taps, heads, size),
        [
            ((width, both + LANES), LOW),
            ((ext, both + LANES), F32),
            ((length, both), F32),
            ((length, both), F32),
            ((length, inner), F32),
            ((inner, half_bc), LOW),
            ((4, length, LANES), F32),
        ],
        place,
        normed,
        x_proj,
        bc_proj,
        dt_wide,
        *first_parts,
        x_conv,
        bc_conv,
        bias_row,
        a_row,
        scratch=[((length, inner), LOW)],
        flops=2 * ext * width * (both + LANES),
    )
    decay = scalars[2, length - 8 :][7:8] * jnp.ones((8, 1), F32)
    other, kept, kept_decay = run_scan(place, state, decay, False, size)
    gate_in, d_no, w_gate, w_out = launch(
        gate_body(fsdp, ctx),
        [
            ((length, inner), F32),
            ((length, inner), LOW),
            ((width, inner), LOW),
            ((inner, width), LOW),
        ],
        place,
        normed,
        cot,
        gate_proj,
        out_proj,
        *gate_parts,
        *out_parts,
        flops=4 * length * width * inner,
    )
    state_in, swept, sums = launch(
        mix_body(last_bit, size),
        [((inner, half_bc), LOW), ((length, inner), F32), ((8, length), F32)],
        place,
        other,
        kept,
        kept_decay,
        act,
        within,
        scalars,
        gate_in,
        d_no,
        skip_row,
        gained,
        flops=2 * length * inner * half_bc,
    )
    others = swap(sums, "tp", 1)
    normed_out, d_gate, d_mixed, d_scaled, state_grad, skip_rows = launch(
        turn_body(size, full_inner),
        [
            ((length, inner), LOW),
            ((length, inner), LOW),
            ((length, inner), F32),
            ((length, inner), LOW),
            ((inner, half_bc), LOW),
            ((8, inner), F32),
        ],
        place,
        sums,
        others,
        act,
        swept,
        scalars,
        gate_in,
        d_no,
        skip_row,
        gained,
        flops=2 * length * inner * half_bc,
    )
    other, kept, kept_decay = run_scan(place, state_grad, decay, True, size)

    w = inner // ctx
    sends = launch(
        deal_body(ctx),
        [((2, length, w), LOW)] * ctx,
        place,
        d_gate,
        normed_out,
        scratch=[((ctx, 2, length, w), LOW)],
        mib=16,
    )
    back, pair_t, half_out, branch = launch(
        local_body(heads, size),
        [
            ((length, inner), F32),
            ((length, length), F32),
            ((length, width), F32),
            ((length, width), LOW),
        ],
        place,
        d_mixed,
        act,
        scalars,
        rows,
        normed_out,
        w_out,
        flops=2 * length * width * inner,
    )
    block_output = (half_out + swap(branch, "tp", 1).astype(F32)).astype(LOW)[None]
    pieces = [sends[0]] + [swap(sends[k], "ctx", k) for k in range(1, ctx)]

    r = 4 * LANES // ctx
    d_first, small, *first_sends = launch(
        rear_body(last_bit, ctx, taps, heads, size),
        [((ext, both + LANES), LOW), ((8, inner), F32)] + [((ext, w + r), LOW)] * ctx,
        place,
        other,
        kept,
        kept_decay,
        back,
        pair_t,
        act,
        conv_out,
        proj,
        scalars,
        swept,
        d_mixed,
        d_scaled,
        state_in,
        skip_row,
        skip_rows,
        x_conv,
        bc_conv,
        bias_row,
        a_row,
        scratch=[
            ((ext + HALO, both), F32),
            ((length, inner), LOW),
            ((length, inner), F32),
            ((length, inner), F32),
            ((ctx, ext, w + r), LOW),
        ],
        flops=2 * length * inner * half_bc * 4,
    )
    first_pieces = [first_sends[0]] + [swap(first_sends[k], "ctx", k) for k in range(1, ctx)]
    own_grad, send_grad, edge, tally = launch(
        down_body,
        [((length, width), F32), ((length, width), LOW), ((HALO, width), LOW), ((8, width), F32)],
        place,
        d_first,
        d_gate,
        w_first,
        w_gate,
        rows,
        halo,
        small,
        flops=2 * ext * width * (both + LANES + inner),
    )
    back_one = [(i + 1, i) for i in range(ctx - 1)]
    edge_in = lax.ppermute(edge, "ctx", back_one)
    edge_peer = swap(edge_in, "tp", 1)
    [input_grad] = launch(
        finish_body,
        [((length, width), F32)],
        place,
        own_grad,
        swap(send_grad, "tp", 1),
        edge_in,
        edge_peer,
        rows,
        cot,
        gain,
        mib=24,
    )

    def reduce_parts(count, columns, *args, stacked):
        span = width // fsdp
        own, *outs = launch(
            weights_body(fsdp, ctx, stacked),
            [((count, columns, span), F32)] + [((count, columns, span), LOW)] * (fsdp - 1),
            place,
            *args,
            scratch=[((count, columns, width), F32)],
            flops=2 * count * columns * width * length * ctx,
        )
        for k in range(1, fsdp):
            own = own + swap(outs[k - 1], "fsdp", k).astype(F32)
        return own.astype(LOW)

    pair_own = reduce_parts(2, w, *pieces, *normed_all, *cot_all, stacked=True)
    pair_all = [pair_own] + [swap(pair_own, "ctx", k) for k in range(1, ctx)]
    first_own = reduce_parts(1, w + r, *first_pieces, *normed_all, stacked=False)
    first_all = [first_own] + [swap(first_own, "ctx", k) for k in range(1, ctx)]
    peer_own = swap(first_own[:, w:], "tp", 1)
    peer_all = [peer_own] + [swap(peer_own, "ctx", k) for k in range(1, ctx)]
    grad_gate, grad_out, grad_x, grad_bc, grad_dt = launch(
        close_body(ctx, inner, states, heads),
        [
            ((shard, inner), F32),
            ((inner, out_proj.shape[1]), F32),
            ((shard, inner), F32),
            ((shard, states), F32),
            ((shard, heads), F32),
        ],
        place,
        *pair_all,
        *first_all,
        *peer_all,
        scratch=[((ctx, w, shard), F32), ((ctx, w, shard), F32), ((2, r * ctx, shard), F32)],
        mib=24,
    )

    shared = (jnp.arange(8) < 2)[:, None]
    tally = tally + jnp.where(shared, swap(tally, "tp", 1), 0.0)
    for axis in ("ctx", "fsdp"):
        for bit in bits_of(axis):
            tally = tally + swap(tally, axis, bit)
    return (
        block_output,
        input_grad[None],
        tally[0],
        grad_gate,
        grad_x,
        grad_bc,
        grad_dt,
        tally[2 : 2 + taps],
        tally[1].reshape(taps, states),
        tally[7, :heads],
        tally[7, LANES : LANES + heads],
        tally[7, 2 * LANES : 2 * LANES + heads],
        tally[6],
        grad_out,
    )


def solution(mesh):
    rows = P("fsdp", "ctx", None)
    both = P("fsdp", "tp")
    head = P("tp")
    in_specs = (
        rows,
        P(),
        both,
        both,
        P("fsdp", None),
        both,
        P(None, "tp"),
        P(),
        head,
        head,
        head,
        head,
        P("tp", "fsdp"),
        rows,
    )
    out_specs = (
        rows,
        rows,
        P(),
        both,
        both,
        P("fsdp", None),
        both,
        P(None, "tp"),
        P(),
        head,
        head,
        head,
        head,
        P("tp", "fsdp"),
    )
    return jax.shard_map(
        on_device, mesh=mesh, in_specs=in_specs, out_specs=out_specs, check_vma=False
    )
```

```python
import jax
import jax.numpy as jnp
from jax import lax
from jax.experimental import pallas as pl
from jax.experimental.pallas import tpu as pltpu
from jax.sharding import PartitionSpec as P

EPSILON = 1e-05
FINE = lax.Precision.HIGHEST
F32 = jnp.float32
LOW = jnp.bfloat16
HALO = 16
LANES = 128
NEVER = -1e30


def swap(block, axis, bits):
    count = lax.axis_size(axis)
    return lax.ppermute(block, axis, [(i, i ^ bits) for i in range(count)])


def bits_of(axis):
    return [1 << b for b in range(lax.axis_size(axis).bit_length() - 1)]


def spread(block, axis):
    pieces = {0: block}
    for bit in reversed(bits_of(axis)):
        pieces.update({k ^ bit: swap(v, axis, bit) for k, v in list(pieces.items())})
    return [pieces[k] for k in range(len(pieces))]


def across_tp(far):
    pairs = {k: [v, swap(v, "tp", 1)] for k, v in far.items()}
    pairs.update({k ^ 1: [swap(h, "ctx", 1) for h in v] for k, v in list(pairs.items())})
    return [h for k in range(2, len(pairs) + 2) for h in pairs[k]]


def far_halves(half):
    far = {0: half}
    for bit in reversed(bits_of("ctx")[1:]):
        far.update({k ^ bit: swap(v, "ctx", bit) for k, v in list(far.items())})
    return {k: v for k, v in far.items() if k}


def launch(body, outs, place, *args, scratch=(), mib=24, deps=(), hbm=(), far=()):
    count = len(args)

    def run(place_ref, *refs):
        body(place_ref, *refs[:count], *refs[count + len(deps) :])

    return pl.pallas_call(
        run,
        out_shape=[jax.ShapeDtypeStruct(s, d) for s, d in outs],
        in_specs=[pl.BlockSpec(memory_space=pltpu.SMEM)]
        + [
            pl.BlockSpec(memory_space=pltpu.HBM if i in hbm else pltpu.VMEM) for i in range(count)
        ]
        + [pl.BlockSpec(memory_space=pl.ANY)] * len(deps),
        out_specs=[
            pl.BlockSpec(memory_space=pltpu.HBM if i in far else pltpu.VMEM)
            for i in range(len(outs))
        ],
        scratch_shapes=[
            pltpu.SemaphoreType.DMA(s) if d is None else pltpu.VMEM(s, d) for s, d in scratch
        ],
        compiler_params=pltpu.CompilerParams(vmem_limit_bytes=mib << 20),
        cost_estimate=pl.CostEstimate(flops=1, bytes_accessed=1, transcendentals=0),
    )(place, *args, *deps)


def aligned(start, count):
    return pl.ds(pl.multiple_of(start, count), count)


def mm(a, b, dims=((1,), (0,))):
    return lax.dot_general(
        a.astype(LOW), b.astype(LOW), (dims, ((), ())), preferred_element_type=F32
    )


NT = ((1,), (1,))
TN = ((0,), (0,))


def fine(a, b):
    return lax.dot_general(
        a, b, (((1,), (0,)), ((), ())), precision=FINE, preferred_element_type=F32
    )


def split_mm(a, b):
    high = a.astype(LOW)
    return mm(high, b) + mm(a - high.astype(F32), b)


def sigmoid(v):
    return 1.0 / (1.0 + jnp.exp(-v))


def silu_slope(v, s):
    return s * (1.0 + v * (1.0 - s))


def iota(shape, dim):
    return lax.broadcasted_iota(jnp.int32, shape, dim)


def pair_wide(v, i, per):
    rows = v.shape[0]
    first = iota((rows, LANES), 1) < LANES // per
    return jnp.where(first, v[:, per * i : per * i + 1], v[:, per * i + 1 : per * i + 2])


def head_of_unit(units, size):
    return iota((units, LANES), 0) // size == iota((units, LANES), 1)


def as_column(row, units, size):
    return jnp.sum(jnp.where(head_of_unit(units, size), row[0:1], 0.0), axis=1, keepdims=True)


def pack_body(place, rows, cot, xp, bcp, dtp, gp, op, packed, edge, dt_wide, halves, sems):
    n = packed.shape[0]
    here = aligned(place[1] * n, n)
    inner, both = xp.shape[1], xp.shape[1] + bcp.shape[1]
    wide = both + LANES
    span = op.shape[1]
    blocks = inner // span
    base = place[1] * n * blocks
    half = aligned(place[2] * halves.shape[1], halves.shape[1])
    moves = [
        (rows.at[rows.shape[0] - HALO :], edge),
        (xp.at[here], packed.at[:, :inner]),
        (bcp.at[here], packed.at[:, inner:both]),
        (gp.at[here], packed.at[:, wide : wide + inner]),
        (rows.at[half], halves.at[0]),
        (cot.at[half], halves.at[1]),
    ]
    for i in range(blocks):
        put = wide + inner + i * span
        moves.append((op.at[aligned(base + i * n, n)], packed.at[:, put : put + span]))
    copies = [pltpu.make_async_copy(a, b, sems.at[i]) for i, (a, b) in enumerate(moves)]
    for copy in copies:
        copy.start()
    turned = dtp[...].astype(F32).T
    blank = jnp.zeros((turned.shape[0], LANES - turned.shape[1]), F32)
    dt_wide[...] = jnp.concatenate([turned, blank], axis=1).astype(LOW)
    packed[:, both:wide] = dt_wide[here, :]
    for copy in copies:
        copy.wait()


def copy_body(place, source, out):
    out[...] = source[...]


def norm_rows(v, gain):
    v = v.astype(F32)
    return v * lax.rsqrt(jnp.mean(v * v, axis=-1, keepdims=True) + EPSILON) * gain


def lay_sequence(place, own, near, halves, which, out):
    length = own.shape[0]
    half = length // 2
    for k, piece in enumerate((own, near)):
        out[aligned((place[1] ^ k) * length, length), :] = piece[...]
    for i, piece in enumerate(halves):
        k, side = 2 + i // 2, i % 2
        at = (place[1] ^ k) * length + (place[2] ^ side) * half
        out[aligned(at, half), :] = piece[which]


def norm_body(place, rows, edge, gain, normed):
    normed[:HALO] = norm_rows(edge[...], gain[...]).astype(LOW)
    for at in range(0, rows.shape[0], 64):
        normed[HALO + at : HALO + at + 64] = norm_rows(rows[at : at + 64], gain[...]).astype(LOW)


def sequence_body(place, gain, rows, near_rows, cot, near_cot, *rest):
    *halves, normed_seq, cot_seq, raw = rest
    normed_seq[:HALO] = jnp.zeros((HALO, raw.shape[1]), LOW)
    lay_sequence(place, rows, near_rows, halves, 0, raw)
    lay_sequence(place, cot, near_cot, halves, 1, cot_seq)

    @pl.loop(0, raw.shape[0] // 64)
    def _(i):
        at = pl.ds(pl.multiple_of(i * 64, 64), 64)
        put = pl.ds(pl.multiple_of(HALO + i * 64, HALO), 64)
        normed_seq[put, :] = norm_rows(raw[at, :], gain[...]).astype(LOW)


def padded(row):
    return jnp.concatenate([row, jnp.zeros((1, LANES - row.shape[1]), F32)], axis=1)


def front_body(fsdp, ctx, taps, heads, size):
    def body(place, normed, xp, bcp, dtp, *rest):
        count = ctx * (fsdp - 1)
        parts = rest[:count]
        x_conv, bc_conv, dt_bias, a_log = rest[count : count + 4]
        w_all, proj, conv_out, act, within, state, scalars, decay, w_x = rest[count + 4 :]
        z, c = place[0], place[1]
        shard, inner = xp.shape
        both = inner + bcp.shape[1]
        half_bc = bcp.shape[1] // 2
        own = aligned(z * shard, shard)
        w_all[own, :inner] = xp[...]
        w_all[own, inner:both] = bcp[...]
        w_all[own, both:] = dtp[...]
        n = shard // ctx
        for j in range(ctx):
            for k in range(1, fsdp):
                put = aligned((z ^ k) * shard + (c ^ j) * n, n)
                w_all[put, :] = parts[j * (fsdp - 1) + k - 1][:, : w_all.shape[1]]
        proj[...] = jnp.dot(normed[...], w_all[...], preferred_element_type=F32)
        length = conv_out.shape[0]
        start = HALO - taps + 1
        for at in range(0, both, LANES):
            cols = slice(at, at + LANES)
            if at < inner:
                tap = x_conv[:, cols]
            else:
                tap = bc_conv[:, at - inner : at - inner + LANES]
            total = tap[0:1] * proj[start : start + length, cols]
            for k in range(1, taps):
                total = total + tap[k : k + 1] * proj[start + k : start + k + length, cols]
            conv_out[:, cols] = total
            act[:, cols] = total * sigmoid(total)
        pre = proj[HALO:, both:] + padded(dt_bias[...])
        step = jnp.maximum(pre, 0.0) + jnp.log1p(jnp.exp(-jnp.abs(pre)))
        log_decay = -jnp.exp(padded(a_log[...])) * step
        lower = iota((length, length), 0) >= iota((length, length), 1)
        cum = fine(jnp.where(lower, 1.0, 0.0), log_decay)
        cum_t = cum.T
        scalars[0] = step
        scalars[1] = cum
        grow = jnp.exp(cum)
        scalars[2] = grow
        decay[...] = jnp.broadcast_to(grow[length - 1 :], decay.shape)
        tail = jnp.exp(cum[length - 1 :] - cum)
        scalars[3] = tail
        b_low = act[:, inner : inner + half_bc].astype(LOW)
        c_low = act[:, inner + half_bc :].astype(LOW)
        scores = mm(c_low, b_low, NT)
        half = length // 2
        per = LANES // size
        first = iota((half, LANES), 1) < size
        for i in range(heads // per):
            cols = slice(LANES * i, LANES * i + LANES)
            stepped = act[:, cols] * pair_wide(step, i, per)
            w_x[:, cols] = (stepped * pair_wide(tail, i, per)).astype(LOW)
            low = stepped.astype(LOW)
            tops, bottoms = [], []
            for h in range(per * i, per * i + per):
                gaps = cum[:half, h : h + 1] - cum_t[h : h + 1, :half]
                top = jnp.exp(jnp.where(lower[:half, :half], gaps, NEVER)) * scores[:half, :half]
                gaps = cum[half:, h : h + 1] - cum_t[h : h + 1, :]
                bottom = jnp.exp(jnp.where(lower[half:], gaps, NEVER)) * scores[half:]
                tops.append(mm(top, low[:half]))
                bottoms.append(mm(bottom, low))
            within[:half, cols] = jnp.where(first, tops[0], tops[1])
            within[half:, cols] = jnp.where(first, bottoms[0], bottoms[1])
        state[...] = mm(w_x[...], b_low, TN).astype(LOW)

    return body


def merge(before, keep, other, decay, other_decay, size):
    units = keep.shape[0]
    earlier = other * as_column(decay, units, size) + keep
    later = keep * as_column(other_decay, units, size) + other
    return jnp.where(before, earlier, later)


def scan_body(bit, reverse, size, first):
    def body(place, state, other, decay, other_decay, *rest):
        if first:
            total, total_decay, prefix, prefix_decay = rest
        else:
            old, old_decay, total, total_decay, prefix, prefix_decay = rest
        before = ((place[1] & bit) != 0) != reverse
        mine, theirs = state[...].astype(F32), other[...].astype(F32)
        total[...] = merge(before, mine, theirs, decay[...], other_decay[...], size).astype(LOW)
        total_decay[...] = decay[...] * other_decay[...]
        if first:
            prefix[...] = jnp.where(before, theirs, 0.0).astype(LOW)
            prefix_decay[...] = jnp.where(before, other_decay[...], 1.0)
        else:
            units = state.shape[0]
            kept = old[...].astype(F32)
            grown = theirs * as_column(old_decay[...], units, size) + kept
            prefix[...] = jnp.where(before, grown, kept).astype(LOW)
            prefix_decay[...] = jnp.where(before, old_decay[...] * other_decay[...], old_decay[...])

    return body


def run_scan(place, state, decay, reverse, size, deps=()):
    bits = bits_of("ctx")
    kept = ()
    for bit in bits[:-1]:
        other, other_decay = swap(state, "ctx", bit), swap(decay, "ctx", bit)
        outs = [(state.shape, LOW), (decay.shape, F32)] * 2
        state, decay, *kept = launch(
            scan_body(bit, reverse, size, not kept),
            outs,
            place,
            state,
            other,
            decay,
            other_decay,
            *kept,
            mib=8,
            deps=deps,
        )
    return swap(state, "ctx", bits[-1]), kept[0], kept[1]


def last_prefix(before, other, kept, kept_decay, size):
    kept_f = kept[...].astype(F32)
    grown = other[...].astype(F32) * as_column(kept_decay[0:1], kept.shape[0], size) + kept_f
    return jnp.where(before, grown, kept_f)


def gate_body(fsdp, ctx):
    def body(place, normed, cot, gp, op, *rest):
        parts = rest[: ctx * (fsdp - 1)]
        gate_in, d_normed_out, w_gate, w_out = rest[ctx * (fsdp - 1) :]
        z, c = place[0], place[1]
        shard = gp.shape[0]
        span, inner = op.shape[1], gp.shape[1]
        w_gate[aligned(z * shard, shard), :] = gp[...]
        w_out[:, aligned(z * span, span)] = op[...]
        n, m = shard // ctx, op.shape[0] // ctx
        wide = parts[0].shape[1] - inner - span * (m // n)
        for j in range(ctx):
            for k in range(1, fsdp):
                part = parts[j * (fsdp - 1) + k - 1]
                w_gate[aligned((z ^ k) * shard + (c ^ j) * n, n), :] = part[:, wide : wide + inner]
                for i in range(m // n):
                    put = wide + inner + i * span
                    w_out[aligned((c ^ j) * m + i * n, n), aligned((z ^ k) * span, span)] = part[
                        :, put : put + span
                    ]
        gate_in[...] = jnp.dot(normed[HALO:], w_gate[...], preferred_element_type=F32)
        d_normed_out[...] = mm(cot[...], w_out[...], NT).astype(LOW)

    return body


def mix_body(bit, size):
    def body(
        place, other, kept, kept_decay, act, within, scalars, gate_in, d_no, skip, gain,
        state_in, swept, sums,
    ):
        before = (place[1] & bit) != 0
        state_in[...] = last_prefix(before, other, kept, kept_decay, size).astype(LOW)
        length, inner = within.shape
        half_bc = (act.shape[1] - inner) // 2
        c_low = act[:, inner + half_bc :].astype(LOW)
        grow = scalars[2]
        per = LANES // size
        squares = jnp.zeros((length, LANES), F32)
        crosses = jnp.zeros((length, LANES), F32)
        for i in range(inner // LANES):
            cols = slice(LANES * i, LANES * i + LANES)
            carried = mm(c_low, state_in[cols, :], NT)
            flow = within[:, cols] + pair_wide(grow, i, per) * carried
            swept[:, cols] = flow
            mixed = flow + pair_wide(skip[...], i, per) * act[:, cols]
            gate = gate_in[:, cols]
            gated = mixed * gate * sigmoid(gate)
            squares = squares + gated * gated
            crosses = crosses + d_no[:, cols].astype(F32) * gain[:, cols] * gated
        lane = iota((length, LANES), 1)
        pair = jnp.where(
            lane == 0,
            jnp.sum(squares, axis=1, keepdims=True),
            jnp.where(lane == 1, jnp.sum(crosses, axis=1, keepdims=True), 0.0),
        )
        sums[...] = pair.T[:8]

    return body


def turn_body(size, full_inner, ctx):
    def body(
        place, mine, theirs, act, swept, scalars, gate_in, d_no, skip, gain,
        normed_out, d_gate, d_mixed, d_scaled, state_grad, rows_out, *rest,
    ):
        length, inner = swept.shape
        half_bc = (act.shape[1] - inner) // 2
        both = (mine[...] + theirs[...]).T
        scale = lax.rsqrt(both[:, 0:1] / full_inner + EPSILON)
        cross = scale * scale * scale / full_inner * both[:, 1:2]
        grow = scalars[2]
        per = LANES // size
        rows_out[...] = jnp.zeros(rows_out.shape, F32)
        for i in range(inner // LANES):
            cols = slice(LANES * i, LANES * i + LANES)
            x_act = act[:, cols]
            mixed = swept[:, cols] + pair_wide(skip[...], i, per) * x_act
            gate = gate_in[:, cols]
            s = sigmoid(gate)
            gated = mixed * gate * s
            grad = d_no[:, cols].astype(F32)
            scaled = gated * scale
            normed_out[:, cols] = (scaled * gain[:, cols]).astype(LOW)
            rows_out[0:1, cols] = jnp.sum(grad * scaled, axis=0, keepdims=True)
            d_gated = scale * gain[:, cols] * grad - gated * cross
            d_gate[:, cols] = (d_gated * mixed * silu_slope(gate, s)).astype(LOW)
            dm = d_gated * gate * s
            d_mixed[:, cols] = dm
            rows_out[1:2, cols] = jnp.sum(dm * x_act, axis=0, keepdims=True)
            d_scaled[:, cols] = (dm * pair_wide(grow, i, per)).astype(LOW)
        c_low = act[:, inner + half_bc :].astype(LOW)
        state_grad[...] = mm(d_scaled[...], c_low, TN).astype(LOW)
        *sends, stage = rest
        w = inner // ctx
        for q in range(ctx):
            stage[q, 0] = d_gate[:, q * w : q * w + w]
            stage[q, 1] = normed_out[:, q * w : q * w + w]
        for k in range(ctx):
            sends[k][...] = stage[place[1] ^ k]

    return body


def local_body(heads, size):
    def body(place, d_mixed, act, scalars, rows, normed_out, w_out, back, pair_t, half_out, branch):
        length, inner = d_mixed.shape
        half_bc = (act.shape[1] - inner) // 2
        out = jnp.dot(normed_out[...], w_out[...], preferred_element_type=F32)
        branch[...] = out.astype(LOW)
        half_out[...] = rows[...].astype(F32) + out
        step, cum = scalars[0], scalars[1]
        cum_t = cum.T
        upper = iota((length, length), 0) <= iota((length, length), 1)
        b_low = act[:, inner : inner + half_bc].astype(LOW)
        c_low = act[:, inner + half_bc :].astype(LOW)
        scores = mm(b_low, c_low, NT)
        half = length // 2
        per = LANES // size
        first = iota((length, LANES), 1) < size
        pair_t[...] = jnp.zeros(pair_t.shape, F32)
        for i in range(heads // per):
            cols = slice(LANES * i, LANES * i + LANES)
            stepped = act[:, cols] * pair_wide(step, i, per)
            grad = d_mixed[:, cols].astype(LOW)
            tops, bottoms = [], []
            for h in range(per * i, per * i + per):
                mask = first if h == per * i else jnp.logical_not(first)
                mine = jnp.where(mask, stepped, 0.0).astype(LOW)
                gaps = cum_t[h : h + 1, :] - cum[:half, h : h + 1]
                top = jnp.exp(jnp.where(upper[:half], gaps, NEVER))
                gaps = cum_t[h : h + 1, half:] - cum[half:, h : h + 1]
                bottom = jnp.exp(jnp.where(upper[half:, half:], gaps, NEVER))
                pair_t[:half] += top * mm(mine[:half], grad, NT)
                pair_t[half:, half:] += bottom * mm(mine[half:], grad[half:], NT)
                tops.append(mm(top * scores[:half], grad))
                bottoms.append(mm(bottom * scores[half:, half:], grad[half:]))
            back[:half, cols] = jnp.where(first[:half], tops[0], tops[1])
            back[half:, cols] = jnp.where(first[:half], bottoms[0], bottoms[1])

    return body


def rear_body(bit, ctx, taps, heads, size):
    def body(
        place, other, kept, kept_decay, back, pair_t, act, conv_out, proj, scalars, swept, d_mixed,
        d_scaled, state_in, skip, skip_rows, x_conv, bc_conv, dt_bias, a_log, *rest,
    ):
        d_first, small = rest[:2]
        sends = rest[2 : 2 + ctx]
        spaced, tails, dots, sweeps, stage = rest[2 + ctx :]
        length, inner = back.shape
        both = act.shape[1]
        half_bc = (both - inner) // 2
        before = (place[1] & bit) == 0
        later_f = last_prefix(before, other, kept, kept_decay, size)
        later = later_f.astype(LOW)
        step, cum, tail = scalars[0], scalars[1], scalars[3]
        b_low = act[:, inner : inner + half_bc].astype(LOW)
        c_low = act[:, inner + half_bc :].astype(LOW)
        per = LANES // size
        ones_at = jnp.where(head_of_unit(inner, size), 1.0, 0.0)
        small[...] = jnp.zeros(small.shape, F32)
        spaced[:HALO] = jnp.zeros((HALO, both), F32)
        spaced[HALO + length :] = jnp.zeros((HALO, both), F32)
        last_rows = []
        for i in range(inner // LANES):
            cols = slice(LANES * i, LANES * i + LANES)
            x_act = act[:, cols]
            wide_step = pair_wide(step, i, per)
            stepped = x_act * wide_step
            wide_tail = pair_wide(tail, i, per)
            tails[:, cols] = (stepped * wide_tail).astype(LOW)
            extra = wide_tail * mm(b_low, later[cols, :], NT)
            last_rows.append(jnp.sum(stepped * extra, axis=0, keepdims=True))
            whole = back[:, cols] + extra
            grad = d_mixed[:, cols]
            dots[:, cols] = x_act * whole
            sweeps[:, cols] = grad * swept[:, cols]
            v = conv_out[:, cols]
            spaced[HALO : HALO + length, cols] = (
                wide_step * whole + pair_wide(skip[...], i, per) * grad
            ) * silu_slope(v, sigmoid(v))
        pair = pair_t[...]
        d_b = mm(pair, c_low) + mm(tails[...], later)
        d_c = mm(pair, b_low, TN) + mm(d_scaled[...], state_in[...])
        for at, d in ((inner, d_b), (inner + half_bc, d_c)):
            v = conv_out[:, at : at + half_bc]
            spaced[HALO : HALO + length, at : at + half_bc] = d * silu_slope(v, sigmoid(v))
        start = HALO - taps + 1
        for at in range(0, both, LANES):
            cols = slice(at, at + LANES)
            if at < inner:
                tap = x_conv[:, cols]
            else:
                tap = bc_conv[:, at - inner : at - inner + LANES]
            grad = spaced[HALO : HALO + length, cols]
            total = tap[0:1] * spaced[taps - 1 : taps - 1 + HALO + length, cols]
            for k in range(1, taps):
                lead = taps - 1 - k
                total = total + tap[k : k + 1] * spaced[lead : lead + HALO + length, cols]
            d_first[:, cols] = total.astype(LOW)
            for k in range(taps):
                found = jnp.sum(
                    grad * proj[start + k : start + k + length, cols], axis=0, keepdims=True
                )
                if at < inner:
                    small[2 + k : 3 + k, cols] = found
                else:
                    put = k * (both - inner) + at - inner
                    small[1:2, put : put + LANES] = found
        d_step = split_mm(dots[...], ones_at)
        row_sum = split_mm(sweeps[...], ones_at)
        cross = jnp.sum(later_f * state_in[...].astype(F32), axis=1, keepdims=True)
        decay_grad = jnp.sum(jnp.where(ones_at > 0, cross, 0.0), axis=0, keepdims=True)
        tail_row = split_mm(
            jnp.broadcast_to(jnp.concatenate(last_rows, axis=1), (8, inner)), ones_at
        )[0:1]
        ends = tail_row + jnp.exp(cum[length - 1 :]) * decay_grad
        upper = jnp.where(iota((length, length), 0) <= iota((length, length), 1), 1.0, 0.0)
        d_log = fine(upper, row_sum - step * d_step) + ends
        rates = jnp.exp(padded(a_log[...]))
        pre = proj[HALO:, both:] + padded(dt_bias[...])
        d_pre = (d_step - rates * d_log) * sigmoid(pre)
        d_pre = jnp.where(iota(d_pre.shape, 1) < heads, d_pre, 0.0)
        d_first[:HALO, both:] = jnp.zeros((HALO, LANES), LOW)
        d_first[HALO:, both:] = d_pre.astype(LOW)
        w = inner // ctx
        blank = 2 * LANES - LANES
        rest_width = both - inner + LANES + blank
        r = rest_width // ctx
        narrow = jnp.concatenate(
            [d_first[:, inner:], jnp.zeros((HALO + length, blank), LOW)], axis=1
        )
        for q in range(ctx):
            stage[q, :, :w] = d_first[:, q * w : q * w + w]
            stage[q, :, w:] = narrow[:, q * r : q * r + r]
        for k in range(ctx):
            sends[k][...] = stage[place[1] ^ k]
        small[6:7] = skip_rows[0:1]
        small[7:8, :LANES] = jnp.sum(d_pre, axis=0, keepdims=True)
        small[7:8, LANES : 2 * LANES] = jnp.sum(
            d_log * (-rates * step), axis=0, keepdims=True
        )
        small[7:8, 2 * LANES : 3 * LANES] = split_mm(
            jnp.broadcast_to(skip_rows[1:2], (8, inner)), ones_at
        )[0:1]

    return body


def down_body(place, d_first, d_gate, w_first, w_gate, rows, halo, small, own, send, edge, tally):
    grad = mm(d_first[...], w_first[...], NT)
    body = grad[HALO:] + mm(d_gate[...], w_gate[...], NT)
    own[...] = body
    send[...] = body.astype(LOW)
    edge[...] = grad[:HALO].astype(LOW)
    tally[...] = small[...]
    total = jnp.sum(grad[:HALO] * norm_rows(halo[...], 1.0), axis=0, keepdims=True)
    for at in range(0, rows.shape[0], 64):
        total = total + jnp.sum(
            body[at : at + 64] * norm_rows(rows[at : at + 64], 1.0), axis=0, keepdims=True
        )
    tally[0:1] = total


def weights_body(fsdp, ctx, stacked):
    def body(place, *rest):
        pieces = rest[:ctx]
        normed_seq = rest[ctx]
        other = rest[ctx + 1] if stacked else None
        keep, send, part = rest[ctx + 2 if stacked else ctx + 1 :]
        length = pieces[0].shape[1] if stacked else pieces[0].shape[0] - HALO
        for j in range(2 if stacked else 1):
            total = None
            for k in range(ctx):
                start = (place[1] ^ k) * length
                if not stacked:
                    big = normed_seq[pl.ds(pl.multiple_of(start, HALO), HALO + length), :]
                    term = mm(pieces[k][...], big, TN)
                else:
                    if j:
                        big = other[pl.ds(pl.multiple_of(start, HALO), length), :]
                    else:
                        big = normed_seq[pl.ds(pl.multiple_of(start + HALO, HALO), length), :]
                    term = mm(pieces[k][j], big, TN)
                total = term if total is None else total + term
            part[j] = total
        span = keep.shape[3]
        for k in range(fsdp):
            block = part[:, :, aligned((place[0] ^ k) * span, span)]
            if k % 2:
                send[k // 2] = block.astype(LOW)
            else:
                keep[k // 2] = block

    return body


def add_body(place, mine, theirs, keep, send):
    for k in range(mine.shape[0]):
        total = mine[k] + theirs[k].astype(F32)
        if k % 2:
            send[k // 2] = total.astype(LOW)
        else:
            keep[k // 2] = total


def last_add_body(place, mine, theirs, *outs):
    total = mine[0] + theirs[0].astype(F32)
    at = 0
    for out in outs:
        out[...] = total[:, at : at + out.shape[1]].astype(LOW)
        at += out.shape[1]


def join_body(states):
    def body(place, mine, theirs, out):
        r = mine.shape[1]
        row = iota(mine.shape, 1) + place[1] * r
        total = mine[...].astype(F32) + jnp.where(row < states, theirs[...].astype(F32), 0.0)
        out[...] = total.astype(LOW)

    return body


def with_tally(body, count, shared=False):
    def run(place, mine, theirs, *rest):
        tally_body(shared)(place, mine, theirs, rest[count])
        body(place, *rest[:count], *rest[count + 1 :])

    return run


def tally_body(shared):
    def body(place, mine, theirs, out):
        if shared:
            row = iota(mine.shape, 0) < 2
            out[...] = mine[...] + jnp.where(row, theirs[...], 0.0)
        else:
            out[...] = mine[...] + theirs[...]

    return body


def small_body(place, mine, theirs, gain, bc_taps, x_taps, gated, bias, decay, skip):
    total = mine[...] + theirs[...]
    gain[...] = total[0:1]
    taps, states = bc_taps.shape
    for k in range(taps):
        bc_taps[k : k + 1] = total[1:2, k * states : k * states + states]
    x_taps[...] = total[2 : 2 + taps]
    gated[...] = total[6:7]
    for i, out in enumerate((bias, decay, skip)):
        out[...] = total[7:8, i * LANES : i * LANES + out.shape[1]]


def output_body(place, half_out, branch, out):
    out[...] = (half_out[...] + branch[...].astype(F32)).astype(LOW)


def close_pair_body(ctx):
    def body(place, *rest):
        pairs = rest[:ctx]
        grad_gate, grad_out, stage = rest[ctx:]
        w = pairs[0].shape[1]
        for k in range(ctx):
            q = place[1] ^ k
            stage[q] = pairs[k][0].astype(F32)
            grad_out[aligned(q * w, w), :] = pairs[k][1].astype(F32)
        for q in range(ctx):
            grad_gate[:, q * w : q * w + w] = stage[q].T

    return body


def close_body(ctx, states, heads):
    def body(place, *rest):
        firsts, lasts = rest[:ctx], rest[ctx : 2 * ctx]
        grad_x, grad_bc, grad_dt, x_stage, r_stage = rest[2 * ctx :]
        r, w = lasts[0].shape[1], firsts[0].shape[1]
        for k in range(ctx):
            q = place[1] ^ k
            x_stage[q] = firsts[k][0].astype(F32)
            r_stage[aligned(q * r, r), :] = lasts[k][0].astype(F32)
        for q in range(ctx):
            grad_x[:, q * w : q * w + w] = x_stage[q].T
        grad_bc[...] = r_stage[:states].T
        grad_dt[...] = r_stage[states : states + heads]

    return body


def finish_body(place, own, peer, edge, edge_peer, rows, cot, gain, out):
    length, width = rows.shape
    extra = edge[...].astype(F32) + edge_peer[...].astype(F32)
    for at in range(0, length, 64):
        v = rows[at : at + 64].astype(F32)
        grad = own[at : at + 64] + peer[at : at + 64].astype(F32)
        if at + 64 == length:
            grad = grad + jnp.concatenate([jnp.zeros((64 - HALO, width), F32), extra])
        scale = lax.rsqrt(jnp.mean(v * v, axis=-1, keepdims=True) + EPSILON)
        d = grad * gain[...]
        inner = jnp.sum(d * v, axis=-1, keepdims=True)
        out[at : at + 64] = (
            cot[at : at + 64].astype(F32)
            + scale * d
            - v * (scale * scale * scale / width * inner)
        )


def on_device(
    block_input,
    input_gain,
    gate_proj,
    x_proj,
    bc_proj,
    dt_proj,
    x_conv,
    bc_conv,
    dt_bias,
    a_log,
    skip_gain,
    gated_gain,
    out_proj,
    cotangent,
):
    length, width = block_input.shape[1:]
    shard, inner = gate_proj.shape
    heads = dt_proj.shape[1]
    size = inner // heads
    states = bc_proj.shape[1]
    half_bc = states // 2
    taps = x_conv.shape[0]
    both = inner + states
    full_inner = inner * lax.axis_size("tp")
    ctx, fsdp = lax.axis_size("ctx"), lax.axis_size("fsdp")
    place = jnp.stack([lax.axis_index(a) for a in ("fsdp", "ctx", "tp")]).astype(jnp.int32)
    rows, cot = block_input[0], cotangent[0]
    ext = HALO + length
    last_bit = bits_of("ctx")[-1]

    gain = input_gain[None]
    wide = both + LANES
    packed, edge_rows, dt_wide, halves = launch(
        pack_body,
        [
            ((shard // ctx, wide + 2 * inner), LOW),
            ((HALO, width), LOW),
            ((shard, LANES), LOW),
            ((2, length // 2, width), LOW),
        ],
        place,
        rows,
        cot,
        x_proj,
        bc_proj,
        dt_proj.T,
        gate_proj,
        out_proj,
        scratch=[((6 + inner // out_proj.shape[1],), None)],
        mib=58,
        hbm=(0, 1, 2, 3, 5, 6),
    )
    halves_far = far_halves(halves)
    halo = lax.ppermute(edge_rows, "ctx", [(i, i + 1) for i in range(ctx - 1)])
    [normed] = launch(norm_body, [((ext, width), LOW)], place, rows, halo, gain, mib=8)
    near = swap(packed, "fsdp", 1)
    [near] = launch(
        copy_body,
        [(packed.shape, LOW)],
        place,
        near,
        mib=4,
        deps=[normed, *halves_far.values()],
    )
    near_y = swap(near, "ctx", bits_of("ctx")[-1])
    found = {0: packed, 1: near}
    for bit in reversed(bits_of("fsdp")[1:]):
        for k in [k for k in found if k % 2 == 0]:
            found[k ^ bit] = swap(found[k], "fsdp", bit)
    for k in [k for k in found if k and k % 2 == 0]:
        [on] = launch(copy_body, [(packed.shape, LOW)], place, found[k], mib=4, deps=[near_y])
        found[k ^ 1] = swap(on, "fsdp", 1)
    far = [found[k] for k in range(1, fsdp)]
    by_distance = [spread(p, "ctx") for p in far]
    parts = [by_distance[k][j] for j in range(ctx) for k in range(fsdp - 1)]
    halves_all = across_tp(halves_far)

    bias_row, a_row, skip_row, gained = (
        dt_bias[None],
        a_log[None],
        skip_gain[None],
        gated_gain[None],
    )
    w_first, proj, conv_out, act, within, state, scalars, decay = launch(
        front_body(fsdp, ctx, taps, heads, size),
        [
            ((width, both + LANES), LOW),
            ((ext, both + LANES), F32),
            ((length, both), F32),
            ((length, both), F32),
            ((length, inner), F32),
            ((inner, half_bc), LOW),
            ((4, length, LANES), F32),
            ((8, LANES), F32),
        ],
        place,
        normed,
        x_proj,
        bc_proj,
        dt_wide,
        *parts,
        x_conv,
        bc_conv,
        bias_row,
        a_row,
        scratch=[((length, inner), LOW)],
    )
    other, kept, kept_decay = run_scan(place, state, decay, False, size, [halves_all[1]])
    gate_in, d_no, w_gate, w_out = launch(
        gate_body(fsdp, ctx),
        [
            ((length, inner), F32),
            ((length, inner), LOW),
            ((width, inner), LOW),
            ((inner, width), LOW),
        ],
        place,
        normed,
        cot,
        gate_proj,
        out_proj,
        *parts,
    )
    normed_seq, cot_seq = launch(
        sequence_body,
        [((HALO + ctx * length, width), LOW), ((ctx * length, width), LOW)],
        place,
        gain,
        rows,
        swap(rows, "ctx", 1),
        cot,
        swap(cot, "ctx", 1),
        *halves_all,
        scratch=[((ctx * length, width), LOW)],
        mib=4 + 10 * ctx // 4,
    )
    state_in, swept, sums = launch(
        mix_body(last_bit, size),
        [((inner, half_bc), LOW), ((length, inner), F32), ((8, length), F32)],
        place,
        other,
        kept,
        kept_decay,
        act,
        within,
        scalars,
        gate_in,
        d_no,
        skip_row,
        gained,
        deps=[normed_seq],
    )
    others = swap(sums, "tp", 1)
    w = inner // ctx
    normed_out, d_gate, d_mixed, d_scaled, state_grad, skip_rows, *sends = launch(
        turn_body(size, full_inner, ctx),
        [
            ((length, inner), LOW),
            ((length, inner), LOW),
            ((length, inner), F32),
            ((length, inner), LOW),
            ((inner, half_bc), LOW),
            ((8, inner), F32),
        ]
        + [((2, length, w), LOW)] * ctx,
        place,
        sums,
        others,
        act,
        swept,
        scalars,
        gate_in,
        d_no,
        skip_row,
        gained,
        scratch=[((ctx, 2, length, w), LOW)],
    )
    other, kept, kept_decay = run_scan(place, state_grad, decay, True, size)

    back, pair_t, half_out, branch = launch(
        local_body(heads, size),
        [
            ((length, inner), F32),
            ((length, length), F32),
            ((length, width), F32),
            ((length, width), LOW),
        ],
        place,
        d_mixed,
        act,
        scalars,
        rows,
        normed_out,
        w_out,
    )
    branch = swap(branch, "tp", 1)
    pieces = [sends[0]] + [swap(sends[k], "ctx", k) for k in range(1, ctx)]

    def partial_sums(count, columns, *args, stacked, deps=()):
        span = width // fsdp
        block = (fsdp // 2, count, columns, span)
        return launch(
            weights_body(fsdp, ctx, stacked),
            [(block, F32), (block, LOW)],
            place,
            *args,
            scratch=[((count, columns, width), F32)],
            mib=20,
            deps=deps,
        )

    def halve(keep, received, deps=()):
        block = (keep.shape[0] // 2, *keep.shape[1:])
        return launch(
            add_body, [(block, F32), (block, LOW)], place, keep, received, mib=10, deps=deps
        )

    pair_keep, pair_send = partial_sums(2, w, *pieces, normed_seq, cot_seq, stacked=True, deps=[other, back])
    pair_send_first = pair_send
    fsdp_bits = bits_of("fsdp")
    received = swap(pair_send, "fsdp", 1)
    for bit in fsdp_bits[1:]:
        pair_keep, pair_send = halve(pair_keep, received)
        received = swap(pair_send, "fsdp", bit)
    r = 4 * LANES // ctx
    d_first, small, *first_sends = launch(
        rear_body(last_bit, ctx, taps, heads, size),
        [((ext, both + LANES), LOW), ((8, inner), F32)] + [((ext, w + r), LOW)] * ctx,
        place,
        other,
        kept,
        kept_decay,
        back,
        pair_t,
        act,
        conv_out,
        proj,
        scalars,
        swept,
        d_mixed,
        d_scaled,
        state_in,
        skip_row,
        skip_rows,
        x_conv,
        bc_conv,
        bias_row,
        a_row,
        scratch=[
            ((ext + HALO, both), F32),
            ((length, inner), LOW),
            ((length, inner), F32),
            ((length, inner), F32),
            ((ctx, ext, w + r), LOW),
        ],
        deps=[pair_send_first],
    )
    first_pieces = [first_sends[0]] + [swap(first_sends[k], "ctx", k) for k in range(1, ctx)]
    own_grad, send_grad, edge, tally = launch(
        down_body,
        [((length, width), F32), ((length, width), LOW), ((HALO, width), LOW), ((8, width), F32)],
        place,
        d_first,
        d_gate,
        w_first,
        w_gate,
        rows,
        halo,
        small,
        deps=[pair_send, branch],
    )

    def add_tally(tally, axis, bit):
        return launch(
            tally_body(axis == "tp"),
            [(tally.shape, F32)],
            place,
            tally,
            swap(tally, axis, bit),
            mib=2,
        )[0]

    high, fsdp_high = bits_of("ctx")[1:], bits_of("fsdp")[1:]
    for hop in [("ctx", b) for b in high[:-1]] + [("fsdp", b) for b in fsdp_high[:-1]]:
        tally = add_tally(tally, *hop)
    [pair_own] = launch(
        last_add_body, [((2, w, width // fsdp), LOW)], place, pair_keep, received, mib=10
    )
    tally, keep, send = launch(
        with_tally(weights_body(fsdp, ctx, False), ctx + 1),
        [
            (tally.shape, F32),
            ((fsdp // 2, 1, w + r, width // fsdp), F32),
            ((fsdp // 2, 1, w + r, width // fsdp), LOW),
        ],
        place,
        tally,
        swap(tally, "ctx", 1),
        *first_pieces,
        normed_seq,
        scratch=[((1, w + r, width), F32)],
        mib=20,
    )
    back_one = [(i + 1, i) for i in range(ctx - 1)]
    edge_in = lax.ppermute(edge, "ctx", back_one)
    edge_peer = swap(edge_in, "tp", 1)
    received = swap(send, "fsdp", 1)
    tally = add_tally(tally, "ctx", high[-1])
    tally_in = swap(tally, "tp", 1)
    [block_output] = launch(
        output_body, [((length, width), LOW)], place, half_out, branch, mib=8
    )
    [input_grad] = launch(
        finish_body,
        [((length, width), F32)],
        place,
        own_grad,
        swap(send_grad, "tp", 1),
        edge_in,
        edge_peer,
        rows,
        cot,
        gain,
        mib=24,
    )
    block = (keep.shape[0] // 2, *keep.shape[1:])
    tally, keep, send = launch(
        with_tally(add_body, 2, True),
        [(tally.shape, F32), (block, F32), (block, LOW)],
        place,
        tally,
        tally_in,
        keep,
        received,
        mib=10,
        deps=[input_grad, block_output],
    )
    received = swap(send, "fsdp", fsdp_bits[1])
    for bit in fsdp_bits[2:]:
        keep, send = halve(keep, received)
        received = swap(send, "fsdp", bit)
    pair_all = [pair_own] + [swap(pair_own, "ctx", k) for k in range(1, ctx)]
    tally, first_own, last_own = launch(
        with_tally(last_add_body, 2),
        [
            (tally.shape, F32),
            ((1, w, width // fsdp), LOW),
            ((1, r, width // fsdp), LOW),
        ],
        place,
        tally,
        swap(tally, "fsdp", 1),
        keep,
        received,
        mib=10,
    )
    first_all = spread(first_own, "ctx")
    [last_own] = launch(
        join_body(states),
        [(last_own.shape, LOW)],
        place,
        last_own,
        swap(last_own, "tp", 1),
        mib=2,
        deps=[first_all[2]],
    )
    last_all = spread(last_own, "ctx")
    grad_gate, grad_out = launch(
        close_pair_body(ctx),
        [((shard, inner), F32), ((inner, out_proj.shape[1]), F32)],
        place,
        *pair_all,
        scratch=[((ctx, w, shard), F32)],
        mib=12,
        deps=[last_all[2]],
    )
    smalls = launch(
        small_body,
        [
            ((1, width), F32),
            ((taps, states), F32),
            ((taps, inner), F32),
            ((1, inner), F32),
            *[((1, heads), F32)] * 3,
        ],
        place,
        tally,
        swap(tally, "fsdp", fsdp_high[-1]),
        mib=2,
    )
    grad_x, grad_bc, grad_dt = launch(
        close_body(ctx, states, heads),
        [((shard, inner), F32), ((shard, states), F32), ((heads, shard), F32)],
        place,
        *first_all,
        *last_all,
        scratch=[((ctx, w, shard), F32), ((r * ctx, shard), F32)],
        mib=12,
    )

    grad_gain, bc_taps, x_taps, grad_gated, grad_bias, grad_a, grad_skip = smalls
    return (
        block_output[None],
        input_grad[None],
        grad_gain[0],
        grad_gate,
        grad_x,
        grad_bc,
        grad_dt.T,
        x_taps,
        bc_taps,
        grad_bias[0],
        grad_a[0],
        grad_skip[0],
        grad_gated[0],
        grad_out,
    )


def solution(mesh):
    rows = P("fsdp", "ctx", None)
    both = P("fsdp", "tp")
    head = P("tp")
    in_specs = (
        rows,
        P(),
        both,
        both,
        P("fsdp", None),
        both,
        P(None, "tp"),
        P(),
        head,
        head,
        head,
        head,
        P("tp", "fsdp"),
        rows,
    )
    out_specs = (
        rows,
        rows,
        P(),
        both,
        both,
        P("fsdp", None),
        both,
        P(None, "tp"),
        P(),
        head,
        head,
        head,
        head,
        P("tp", "fsdp"),
    )
    return jax.shard_map(
        on_device, mesh=mesh, in_specs=in_specs, out_specs=out_specs, check_vma=False
    )
```

```python
import jax
import jax.numpy as jnp
from jax import lax
from jax.experimental import pallas as pl
from jax.experimental.pallas import tpu as pltpu
from jax.sharding import PartitionSpec as P

EPSILON = 1e-05
FINE = lax.Precision.HIGHEST
F32 = jnp.float32
LOW = jnp.bfloat16
HALO = 16
LANES = 128
NEVER = -1e30


def swap(block, axis, bits):
    count = lax.axis_size(axis)
    return lax.ppermute(block, axis, [(i, i ^ bits) for i in range(count)])


def bits_of(axis):
    return [1 << b for b in range(lax.axis_size(axis).bit_length() - 1)]


def spread(block, axis):
    pieces = {0: block}
    for bit in reversed(bits_of(axis)):
        pieces.update({k ^ bit: swap(v, axis, bit) for k, v in list(pieces.items())})
    return [pieces[k] for k in range(len(pieces))]


def across_tp(far):
    pairs = {k: [v, swap(v, "tp", 1)] for k, v in far.items()}
    pairs.update({k ^ 1: [swap(h, "ctx", 1) for h in v] for k, v in list(pairs.items())})
    return [h for k in range(2, len(pairs) + 2) for h in pairs[k]]


def far_halves(half):
    far = {0: half}
    for bit in reversed(bits_of("ctx")[1:]):
        far.update({k ^ bit: swap(v, "ctx", bit) for k, v in list(far.items())})
    return {k: v for k, v in far.items() if k}


def launch(body, outs, place, *args, scratch=(), mib=24, deps=(), hbm=(), far=()):
    count = len(args)

    def run(place_ref, *refs):
        body(place_ref, *refs[:count], *refs[count + len(deps) :])

    return pl.pallas_call(
        run,
        out_shape=[jax.ShapeDtypeStruct(s, d) for s, d in outs],
        in_specs=[pl.BlockSpec(memory_space=pltpu.SMEM)]
        + [
            pl.BlockSpec(memory_space=pltpu.HBM if i in hbm else pltpu.VMEM) for i in range(count)
        ]
        + [pl.BlockSpec(memory_space=pl.ANY)] * len(deps),
        out_specs=[
            pl.BlockSpec(memory_space=pltpu.HBM if i in far else pltpu.VMEM)
            for i in range(len(outs))
        ],
        scratch_shapes=[
            pltpu.SemaphoreType.DMA(s) if d is None else pltpu.VMEM(s, d) for s, d in scratch
        ],
        compiler_params=pltpu.CompilerParams(vmem_limit_bytes=mib << 20),
        cost_estimate=pl.CostEstimate(flops=1, bytes_accessed=1, transcendentals=0),
    )(place, *args, *deps)


def aligned(start, count):
    return pl.ds(pl.multiple_of(start, count), count)


def mm(a, b, dims=((1,), (0,))):
    return lax.dot_general(
        a.astype(LOW), b.astype(LOW), (dims, ((), ())), preferred_element_type=F32
    )


NT = ((1,), (1,))
TN = ((0,), (0,))


def fine(a, b):
    return lax.dot_general(
        a, b, (((1,), (0,)), ((), ())), precision=FINE, preferred_element_type=F32
    )


def split_mm(a, b):
    high = a.astype(LOW)
    return mm(high, b) + mm(a - high.astype(F32), b)


def sigmoid(v):
    return 1.0 / (1.0 + jnp.exp(-v))


def silu_slope(v, s):
    return s * (1.0 + v * (1.0 - s))


def iota(shape, dim):
    return lax.broadcasted_iota(jnp.int32, shape, dim)


def pair_wide(v, i, per):
    rows = v.shape[0]
    first = iota((rows, LANES), 1) < LANES // per
    return jnp.where(first, v[:, per * i : per * i + 1], v[:, per * i + 1 : per * i + 2])


def head_of_unit(units, size):
    return iota((units, LANES), 0) // size == iota((units, LANES), 1)


def as_column(row, units, size):
    return jnp.sum(jnp.where(head_of_unit(units, size), row[0:1], 0.0), axis=1, keepdims=True)


def pack_body(place, rows, cot, xp, bcp, dtp, gp, op, packed, edge, dt_wide, halves, sems):
    n = packed.shape[0]
    here = aligned(place[1] * n, n)
    inner, both = xp.shape[1], xp.shape[1] + bcp.shape[1]
    wide = both + LANES
    span = op.shape[1]
    blocks = inner // span
    base = place[1] * n * blocks
    half = aligned(place[2] * halves.shape[1], halves.shape[1])
    moves = [
        (rows.at[rows.shape[0] - HALO :], edge),
        (xp.at[here], packed.at[:, :inner]),
        (bcp.at[here], packed.at[:, inner:both]),
        (gp.at[here], packed.at[:, wide : wide + inner]),
        (rows.at[half], halves.at[0]),
        (cot.at[half], halves.at[1]),
    ]
    for i in range(blocks):
        put = wide + inner + i * span
        moves.append((op.at[aligned(base + i * n, n)], packed.at[:, put : put + span]))
    copies = [pltpu.make_async_copy(a, b, sems.at[i]) for i, (a, b) in enumerate(moves)]
    for copy in copies:
        copy.start()
    turned = dtp[...].astype(F32).T
    blank = jnp.zeros((turned.shape[0], LANES - turned.shape[1]), F32)
    dt_wide[...] = jnp.concatenate([turned, blank], axis=1).astype(LOW)
    packed[:, both:wide] = dt_wide[here, :]
    for copy in copies:
        copy.wait()


def copy_body(place, source, out):
    out[...] = source[...]


def norm_rows(v, gain):
    v = v.astype(F32)
    return v * lax.rsqrt(jnp.mean(v * v, axis=-1, keepdims=True) + EPSILON) * gain


def lay_sequence(place, own, near, halves, which, out):
    length = own.shape[0]
    half = length // 2
    for k, piece in enumerate((own, near)):
        out[aligned((place[1] ^ k) * length, length), :] = piece[...]
    for i, piece in enumerate(halves):
        k, side = 2 + i // 2, i % 2
        at = (place[1] ^ k) * length + (place[2] ^ side) * half
        out[aligned(at, half), :] = piece[which]


def norm_body(place, rows, edge, gain, normed):
    normed[:HALO] = norm_rows(edge[...], gain[...]).astype(LOW)
    for at in range(0, rows.shape[0], 64):
        normed[HALO + at : HALO + at + 64] = norm_rows(rows[at : at + 64], gain[...]).astype(LOW)


def sequence_body(place, gain, rows, near_rows, cot, near_cot, *rest):
    *halves, normed_seq, cot_seq, raw = rest
    normed_seq[:HALO] = jnp.zeros((HALO, raw.shape[1]), LOW)
    lay_sequence(place, rows, near_rows, halves, 0, raw)
    lay_sequence(place, cot, near_cot, halves, 1, cot_seq)

    @pl.loop(0, raw.shape[0] // 64)
    def _(i):
        at = pl.ds(pl.multiple_of(i * 64, 64), 64)
        put = pl.ds(pl.multiple_of(HALO + i * 64, HALO), 64)
        normed_seq[put, :] = norm_rows(raw[at, :], gain[...]).astype(LOW)


def padded(row):
    return jnp.concatenate([row, jnp.zeros((1, LANES - row.shape[1]), F32)], axis=1)


def front_body(fsdp, ctx, taps, heads, size):
    def body(place, normed, xp, bcp, dtp, *rest):
        count = ctx * (fsdp - 1)
        parts = rest[:count]
        x_conv, bc_conv, dt_bias, a_log = rest[count : count + 4]
        w_all, proj, conv_out, act, within, state, scalars, decay, w_x = rest[count + 4 :]
        z, c = place[0], place[1]
        shard, inner = xp.shape
        both = inner + bcp.shape[1]
        half_bc = bcp.shape[1] // 2
        own = aligned(z * shard, shard)
        w_all[own, :inner] = xp[...]
        w_all[own, inner:both] = bcp[...]
        w_all[own, both:] = dtp[...]
        n = shard // ctx
        for j in range(ctx):
            for k in range(1, fsdp):
                put = aligned((z ^ k) * shard + (c ^ j) * n, n)
                w_all[put, :] = parts[j * (fsdp - 1) + k - 1][:, : w_all.shape[1]]
        proj[...] = jnp.dot(normed[...], w_all[...], preferred_element_type=F32)
        length = conv_out.shape[0]
        start = HALO - taps + 1
        for at in range(0, both, LANES):
            cols = slice(at, at + LANES)
            if at < inner:
                tap = x_conv[:, cols]
            else:
                tap = bc_conv[:, at - inner : at - inner + LANES]
            total = tap[0:1] * proj[start : start + length, cols]
            for k in range(1, taps):
                total = total + tap[k : k + 1] * proj[start + k : start + k + length, cols]
            conv_out[:, cols] = total
            act[:, cols] = total * sigmoid(total)
        pre = proj[HALO:, both:] + padded(dt_bias[...])
        step = jnp.maximum(pre, 0.0) + jnp.log1p(jnp.exp(-jnp.abs(pre)))
        log_decay = -jnp.exp(padded(a_log[...])) * step
        lower = iota((length, length), 0) >= iota((length, length), 1)
        cum = fine(jnp.where(lower, 1.0, 0.0), log_decay)
        cum_t = cum.T
        scalars[0] = step
        scalars[1] = cum
        grow = jnp.exp(cum)
        scalars[2] = grow
        decay[...] = jnp.broadcast_to(grow[length - 1 :], decay.shape)
        tail = jnp.exp(cum[length - 1 :] - cum)
        scalars[3] = tail
        b_low = act[:, inner : inner + half_bc].astype(LOW)
        c_low = act[:, inner + half_bc :].astype(LOW)
        scores = mm(c_low, b_low, NT)
        half = length // 2
        per = LANES // size
        first = iota((half, LANES), 1) < size
        for i in range(heads // per):
            cols = slice(LANES * i, LANES * i + LANES)
            stepped = act[:, cols] * pair_wide(step, i, per)
            w_x[:, cols] = (stepped * pair_wide(tail, i, per)).astype(LOW)
            low = stepped.astype(LOW)
            tops, bottoms = [], []
            for h in range(per * i, per * i + per):
                gaps = cum[:half, h : h + 1] - cum_t[h : h + 1, :half]
                top = jnp.exp(jnp.where(lower[:half, :half], gaps, NEVER)) * scores[:half, :half]
                gaps = cum[half:, h : h + 1] - cum_t[h : h + 1, :]
                bottom = jnp.exp(jnp.where(lower[half:], gaps, NEVER)) * scores[half:]
                tops.append(mm(top, low[:half]))
                bottoms.append(mm(bottom, low))
            within[:half, cols] = jnp.where(first, tops[0], tops[1])
            within[half:, cols] = jnp.where(first, bottoms[0], bottoms[1])
        state[...] = mm(w_x[...], b_low, TN).astype(LOW)

    return body


def merge(before, keep, other, decay, other_decay, size):
    units = keep.shape[0]
    earlier = other * as_column(decay, units, size) + keep
    later = keep * as_column(other_decay, units, size) + other
    return jnp.where(before, earlier, later)


def scan_body(bit, reverse, size, first):
    def body(place, state, other, decay, other_decay, *rest):
        if first:
            total, total_decay, prefix, prefix_decay = rest
        else:
            old, old_decay, total, total_decay, prefix, prefix_decay = rest
        before = ((place[1] & bit) != 0) != reverse
        mine, theirs = state[...].astype(F32), other[...].astype(F32)
        total[...] = merge(before, mine, theirs, decay[...], other_decay[...], size).astype(LOW)
        total_decay[...] = decay[...] * other_decay[...]
        if first:
            prefix[...] = jnp.where(before, theirs, 0.0).astype(LOW)
            prefix_decay[...] = jnp.where(before, other_decay[...], 1.0)
        else:
            units = state.shape[0]
            kept = old[...].astype(F32)
            grown = theirs * as_column(old_decay[...], units, size) + kept
            prefix[...] = jnp.where(before, grown, kept).astype(LOW)
            prefix_decay[...] = jnp.where(before, old_decay[...] * other_decay[...], old_decay[...])

    return body


def run_scan(place, state, decay, reverse, size, deps=()):
    bits = bits_of("ctx")
    kept = ()
    for bit in bits[:-1]:
        other, other_decay = swap(state, "ctx", bit), swap(decay, "ctx", bit)
        outs = [(state.shape, LOW), (decay.shape, F32)] * 2
        state, decay, *kept = launch(
            scan_body(bit, reverse, size, not kept),
            outs,
            place,
            state,
            other,
            decay,
            other_decay,
            *kept,
            mib=8,
            deps=deps,
        )
    return swap(state, "ctx", bits[-1]), kept[0], kept[1]


def last_prefix(before, other, kept, kept_decay, size):
    kept_f = kept[...].astype(F32)
    grown = other[...].astype(F32) * as_column(kept_decay[0:1], kept.shape[0], size) + kept_f
    return jnp.where(before, grown, kept_f)


def gate_body(fsdp, ctx):
    def body(place, normed, cot, gp, op, *rest):
        parts = rest[: ctx * (fsdp - 1)]
        gate_in, d_normed_out, w_gate, w_out = rest[ctx * (fsdp - 1) :]
        z, c = place[0], place[1]
        shard = gp.shape[0]
        span, inner = op.shape[1], gp.shape[1]
        w_gate[aligned(z * shard, shard), :] = gp[...]
        w_out[:, aligned(z * span, span)] = op[...]
        n, m = shard // ctx, op.shape[0] // ctx
        wide = parts[0].shape[1] - inner - span * (m // n)
        for j in range(ctx):
            for k in range(1, fsdp):
                part = parts[j * (fsdp - 1) + k - 1]
                w_gate[aligned((z ^ k) * shard + (c ^ j) * n, n), :] = part[:, wide : wide + inner]
                for i in range(m // n):
                    put = wide + inner + i * span
                    w_out[aligned((c ^ j) * m + i * n, n), aligned((z ^ k) * span, span)] = part[
                        :, put : put + span
                    ]
        gate_in[...] = jnp.dot(normed[HALO:], w_gate[...], preferred_element_type=F32)
        d_normed_out[...] = mm(cot[...], w_out[...], NT).astype(LOW)

    return body


def mix_body(bit, size):
    def body(
        place, other, kept, kept_decay, act, within, scalars, gate_in, d_no, skip, gain,
        state_in, swept, sums,
    ):
        before = (place[1] & bit) != 0
        state_in[...] = last_prefix(before, other, kept, kept_decay, size).astype(LOW)
        length, inner = within.shape
        half_bc = (act.shape[1] - inner) // 2
        c_low = act[:, inner + half_bc :].astype(LOW)
        grow = scalars[2]
        per = LANES // size
        squares = jnp.zeros((length, LANES), F32)
        crosses = jnp.zeros((length, LANES), F32)
        for i in range(inner // LANES):
            cols = slice(LANES * i, LANES * i + LANES)
            carried = mm(c_low, state_in[cols, :], NT)
            flow = within[:, cols] + pair_wide(grow, i, per) * carried
            swept[:, cols] = flow
            mixed = flow + pair_wide(skip[...], i, per) * act[:, cols]
            gate = gate_in[:, cols]
            gated = mixed * gate * sigmoid(gate)
            squares = squares + gated * gated
            crosses = crosses + d_no[:, cols].astype(F32) * gain[:, cols] * gated
        lane = iota((length, LANES), 1)
        pair = jnp.where(
            lane == 0,
            jnp.sum(squares, axis=1, keepdims=True),
            jnp.where(lane == 1, jnp.sum(crosses, axis=1, keepdims=True), 0.0),
        )
        sums[...] = pair.T[:8]

    return body


def turn_body(size, full_inner, ctx):
    def body(
        place, mine, theirs, act, swept, scalars, gate_in, d_no, skip, gain,
        normed_out, d_gate, d_mixed, d_scaled, state_grad, rows_out, *rest,
    ):
        length, inner = swept.shape
        half_bc = (act.shape[1] - inner) // 2
        both = (mine[...] + theirs[...]).T
        scale = lax.rsqrt(both[:, 0:1] / full_inner + EPSILON)
        cross = scale * scale * scale / full_inner * both[:, 1:2]
        grow = scalars[2]
        per = LANES // size
        rows_out[...] = jnp.zeros(rows_out.shape, F32)
        for i in range(inner // LANES):
            cols = slice(LANES * i, LANES * i + LANES)
            x_act = act[:, cols]
            mixed = swept[:, cols] + pair_wide(skip[...], i, per) * x_act
            gate = gate_in[:, cols]
            s = sigmoid(gate)
            gated = mixed * gate * s
            grad = d_no[:, cols].astype(F32)
            scaled = gated * scale
            normed_out[:, cols] = (scaled * gain[:, cols]).astype(LOW)
            rows_out[0:1, cols] = jnp.sum(grad * scaled, axis=0, keepdims=True)
            d_gated = scale * gain[:, cols] * grad - gated * cross
            d_gate[:, cols] = (d_gated * mixed * silu_slope(gate, s)).astype(LOW)
            dm = d_gated * gate * s
            d_mixed[:, cols] = dm
            rows_out[1:2, cols] = jnp.sum(dm * x_act, axis=0, keepdims=True)
            d_scaled[:, cols] = (dm * pair_wide(grow, i, per)).astype(LOW)
        c_low = act[:, inner + half_bc :].astype(LOW)
        state_grad[...] = mm(d_scaled[...], c_low, TN).astype(LOW)
        *sends, stage = rest
        w = inner // ctx
        for q in range(ctx):
            stage[q, 0] = d_gate[:, q * w : q * w + w]
            stage[q, 1] = normed_out[:, q * w : q * w + w]
        for k in range(ctx):
            sends[k][...] = stage[place[1] ^ k]

    return body


def local_body(heads, size):
    def body(place, d_mixed, act, scalars, rows, normed_out, w_out, back, pair_t, half_out, branch):
        length, inner = d_mixed.shape
        half_bc = (act.shape[1] - inner) // 2
        out = jnp.dot(normed_out[...], w_out[...], preferred_element_type=F32)
        branch[...] = out.astype(LOW)
        half_out[...] = rows[...].astype(F32) + out
        step, cum = scalars[0], scalars[1]
        cum_t = cum.T
        upper = iota((length, length), 0) <= iota((length, length), 1)
        b_low = act[:, inner : inner + half_bc].astype(LOW)
        c_low = act[:, inner + half_bc :].astype(LOW)
        scores = mm(b_low, c_low, NT)
        half = length // 2
        per = LANES // size
        first = iota((length, LANES), 1) < size
        pair_t[...] = jnp.zeros(pair_t.shape, F32)
        for i in range(heads // per):
            cols = slice(LANES * i, LANES * i + LANES)
            stepped = act[:, cols] * pair_wide(step, i, per)
            grad = d_mixed[:, cols].astype(LOW)
            tops, bottoms = [], []
            for h in range(per * i, per * i + per):
                mask = first if h == per * i else jnp.logical_not(first)
                mine = jnp.where(mask, stepped, 0.0).astype(LOW)
                gaps = cum_t[h : h + 1, :] - cum[:half, h : h + 1]
                top = jnp.exp(jnp.where(upper[:half], gaps, NEVER))
                gaps = cum_t[h : h + 1, half:] - cum[half:, h : h + 1]
                bottom = jnp.exp(jnp.where(upper[half:, half:], gaps, NEVER))
                pair_t[:half] += top * mm(mine[:half], grad, NT)
                pair_t[half:, half:] += bottom * mm(mine[half:], grad[half:], NT)
                tops.append(mm(top * scores[:half], grad))
                bottoms.append(mm(bottom * scores[half:, half:], grad[half:]))
            back[:half, cols] = jnp.where(first[:half], tops[0], tops[1])
            back[half:, cols] = jnp.where(first[:half], bottoms[0], bottoms[1])

    return body


def rear_body(bit, ctx, taps, heads, size):
    def body(
        place, other, kept, kept_decay, back, pair_t, act, conv_out, proj, scalars, swept, d_mixed,
        d_scaled, state_in, skip, skip_rows, x_conv, bc_conv, dt_bias, a_log, *rest,
    ):
        d_first, small = rest[:2]
        sends = rest[2 : 2 + ctx]
        spaced, tails, dots, sweeps, stage = rest[2 + ctx :]
        length, inner = back.shape
        both = act.shape[1]
        half_bc = (both - inner) // 2
        before = (place[1] & bit) == 0
        later_f = last_prefix(before, other, kept, kept_decay, size)
        later = later_f.astype(LOW)
        step, cum, tail = scalars[0], scalars[1], scalars[3]
        b_low = act[:, inner : inner + half_bc].astype(LOW)
        c_low = act[:, inner + half_bc :].astype(LOW)
        per = LANES // size
        ones_at = jnp.where(head_of_unit(inner, size), 1.0, 0.0)
        small[...] = jnp.zeros(small.shape, F32)
        spaced[:HALO] = jnp.zeros((HALO, both), F32)
        spaced[HALO + length :] = jnp.zeros((HALO, both), F32)
        last_rows = []
        for i in range(inner // LANES):
            cols = slice(LANES * i, LANES * i + LANES)
            x_act = act[:, cols]
            wide_step = pair_wide(step, i, per)
            stepped = x_act * wide_step
            wide_tail = pair_wide(tail, i, per)
            tails[:, cols] = (stepped * wide_tail).astype(LOW)
            extra = wide_tail * mm(b_low, later[cols, :], NT)
            last_rows.append(jnp.sum(stepped * extra, axis=0, keepdims=True))
            whole = back[:, cols] + extra
            grad = d_mixed[:, cols]
            dots[:, cols] = x_act * whole
            sweeps[:, cols] = grad * swept[:, cols]
            v = conv_out[:, cols]
            spaced[HALO : HALO + length, cols] = (
                wide_step * whole + pair_wide(skip[...], i, per) * grad
            ) * silu_slope(v, sigmoid(v))
        pair = pair_t[...]
        d_b = mm(pair, c_low) + mm(tails[...], later)
        d_c = mm(pair, b_low, TN) + mm(d_scaled[...], state_in[...])
        for at, d in ((inner, d_b), (inner + half_bc, d_c)):
            v = conv_out[:, at : at + half_bc]
            spaced[HALO : HALO + length, at : at + half_bc] = d * silu_slope(v, sigmoid(v))
        start = HALO - taps + 1
        for at in range(0, both, LANES):
            cols = slice(at, at + LANES)
            if at < inner:
                tap = x_conv[:, cols]
            else:
                tap = bc_conv[:, at - inner : at - inner + LANES]
            grad = spaced[HALO : HALO + length, cols]
            total = tap[0:1] * spaced[taps - 1 : taps - 1 + HALO + length, cols]
            for k in range(1, taps):
                lead = taps - 1 - k
                total = total + tap[k : k + 1] * spaced[lead : lead + HALO + length, cols]
            d_first[:, cols] = total.astype(LOW)
            for k in range(taps):
                found = jnp.sum(
                    grad * proj[start + k : start + k + length, cols], axis=0, keepdims=True
                )
                if at < inner:
                    small[2 + k : 3 + k, cols] = found
                else:
                    put = k * (both - inner) + at - inner
                    small[1:2, put : put + LANES] = found
        d_step = split_mm(dots[...], ones_at)
        row_sum = split_mm(sweeps[...], ones_at)
        cross = jnp.sum(later_f * state_in[...].astype(F32), axis=1, keepdims=True)
        decay_grad = jnp.sum(jnp.where(ones_at > 0, cross, 0.0), axis=0, keepdims=True)
        tail_row = split_mm(
            jnp.broadcast_to(jnp.concatenate(last_rows, axis=1), (8, inner)), ones_at
        )[0:1]
        ends = tail_row + jnp.exp(cum[length - 1 :]) * decay_grad
        upper = jnp.where(iota((length, length), 0) <= iota((length, length), 1), 1.0, 0.0)
        d_log = fine(upper, row_sum - step * d_step) + ends
        rates = jnp.exp(padded(a_log[...]))
        pre = proj[HALO:, both:] + padded(dt_bias[...])
        d_pre = (d_step - rates * d_log) * sigmoid(pre)
        d_pre = jnp.where(iota(d_pre.shape, 1) < heads, d_pre, 0.0)
        d_first[:HALO, both:] = jnp.zeros((HALO, LANES), LOW)
        d_first[HALO:, both:] = d_pre.astype(LOW)
        w = inner // ctx
        blank = 2 * LANES - LANES
        rest_width = both - inner + LANES + blank
        r = rest_width // ctx
        narrow = jnp.concatenate(
            [d_first[:, inner:], jnp.zeros((HALO + length, blank), LOW)], axis=1
        )
        for q in range(ctx):
            stage[q, :, :w] = d_first[:, q * w : q * w + w]
            stage[q, :, w:] = narrow[:, q * r : q * r + r]
        for k in range(ctx):
            sends[k][...] = stage[place[1] ^ k]
        small[6:7] = skip_rows[0:1]
        small[7:8, :LANES] = jnp.sum(d_pre, axis=0, keepdims=True)
        small[7:8, LANES : 2 * LANES] = jnp.sum(
            d_log * (-rates * step), axis=0, keepdims=True
        )
        small[7:8, 2 * LANES : 3 * LANES] = split_mm(
            jnp.broadcast_to(skip_rows[1:2], (8, inner)), ones_at
        )[0:1]

    return body


def down_body(place, d_first, d_gate, w_first, w_gate, rows, halo, small, own, send, edge, tally):
    grad = mm(d_first[...], w_first[...], NT)
    body = grad[HALO:] + mm(d_gate[...], w_gate[...], NT)
    own[...] = body
    send[...] = body.astype(LOW)
    edge[...] = grad[:HALO].astype(LOW)
    tally[...] = small[...]
    total = jnp.sum(grad[:HALO] * norm_rows(halo[...], 1.0), axis=0, keepdims=True)
    for at in range(0, rows.shape[0], 64):
        total = total + jnp.sum(
            body[at : at + 64] * norm_rows(rows[at : at + 64], 1.0), axis=0, keepdims=True
        )
    tally[0:1] = total


def weights_body(fsdp, ctx, stacked):
    def body(place, *rest):
        pieces = rest[:ctx]
        normed_seq = rest[ctx]
        other = rest[ctx + 1] if stacked else None
        keep, send, part = rest[ctx + 2 if stacked else ctx + 1 :]
        length = pieces[0].shape[1] if stacked else pieces[0].shape[0] - HALO
        for j in range(2 if stacked else 1):
            total = None
            for k in range(ctx):
                start = (place[1] ^ k) * length
                if not stacked:
                    big = normed_seq[pl.ds(pl.multiple_of(start, HALO), HALO + length), :]
                    term = mm(pieces[k][...], big, TN)
                else:
                    if j:
                        big = other[pl.ds(pl.multiple_of(start, HALO), length), :]
                    else:
                        big = normed_seq[pl.ds(pl.multiple_of(start + HALO, HALO), length), :]
                    term = mm(pieces[k][j], big, TN)
                total = term if total is None else total + term
            part[j] = total
        span = keep.shape[3]
        for k in range(fsdp):
            block = part[:, :, aligned((place[0] ^ k) * span, span)]
            if k % 2:
                send[k // 2] = block.astype(LOW)
            else:
                keep[k // 2] = block

    return body


def add_body(place, mine, theirs, keep, send):
    for k in range(mine.shape[0]):
        total = mine[k] + theirs[k].astype(F32)
        if k % 2:
            send[k // 2] = total.astype(LOW)
        else:
            keep[k // 2] = total


def last_add_body(place, mine, theirs, *outs):
    total = mine[0] + theirs[0].astype(F32)
    at = 0
    for out in outs:
        out[...] = total[:, at : at + out.shape[1]].astype(LOW)
        at += out.shape[1]


def join_body(states):
    def body(place, mine, theirs, out):
        r = mine.shape[1]
        row = iota(mine.shape, 1) + place[1] * r
        total = mine[...].astype(F32) + jnp.where(row < states, theirs[...].astype(F32), 0.0)
        out[...] = total.astype(LOW)

    return body


def with_tally(body, count, shared=False):
    def run(place, mine, theirs, *rest):
        tally_body(shared)(place, mine, theirs, rest[count])
        body(place, *rest[:count], *rest[count + 1 :])

    return run


def tally_body(shared):
    def body(place, mine, theirs, out):
        if shared:
            row = iota(mine.shape, 0) < 2
            out[...] = mine[...] + jnp.where(row, theirs[...], 0.0)
        else:
            out[...] = mine[...] + theirs[...]

    return body


def small_body(place, mine, theirs, gain, bc_taps, x_taps, gated, bias, decay, skip):
    total = mine[...] + theirs[...]
    gain[...] = total[0:1]
    taps, states = bc_taps.shape
    for k in range(taps):
        bc_taps[k : k + 1] = total[1:2, k * states : k * states + states]
    x_taps[...] = total[2 : 2 + taps]
    gated[...] = total[6:7]
    for i, out in enumerate((bias, decay, skip)):
        out[...] = total[7:8, i * LANES : i * LANES + out.shape[1]]


def end_body(ctx, states, heads):
    def body(place, *rest):
        ins, rest = rest[: 3 * ctx + 2], rest[3 * ctx + 2 :]
        outs, stages = rest[:12], rest[12:]
        close_pair_body(ctx)(place, *ins[:ctx], *outs[:2], stages[0])
        close_body(ctx, states, heads)(place, *ins[ctx : 3 * ctx], *outs[2:5], *stages[1:])
        small_body(place, *ins[3 * ctx :], *outs[5:])

    return body


def output_body(place, half_out, branch, out):
    out[...] = (half_out[...] + branch[...].astype(F32)).astype(LOW)


def close_pair_body(ctx):
    def body(place, *rest):
        pairs = rest[:ctx]
        grad_gate, grad_out, stage = rest[ctx:]
        w = pairs[0].shape[1]
        for k in range(ctx):
            q = place[1] ^ k
            stage[q] = pairs[k][0].astype(F32)
            grad_out[aligned(q * w, w), :] = pairs[k][1].astype(F32)
        for q in range(ctx):
            grad_gate[:, q * w : q * w + w] = stage[q].T

    return body


def close_body(ctx, states, heads):
    def body(place, *rest):
        firsts, lasts = rest[:ctx], rest[ctx : 2 * ctx]
        grad_x, grad_bc, grad_dt, x_stage, r_stage = rest[2 * ctx :]
        r, w = lasts[0].shape[1], firsts[0].shape[1]
        for k in range(ctx):
            q = place[1] ^ k
            x_stage[q] = firsts[k][0].astype(F32)
            r_stage[aligned(q * r, r), :] = lasts[k][0].astype(F32)
        for q in range(ctx):
            grad_x[:, q * w : q * w + w] = x_stage[q].T
        grad_bc[...] = r_stage[:states].T
        grad_dt[...] = r_stage[states : states + heads]

    return body


def finish_body(place, own, peer, edge, edge_peer, rows, cot, gain, out):
    length, width = rows.shape
    extra = edge[...].astype(F32) + edge_peer[...].astype(F32)
    for at in range(0, length, 64):
        v = rows[at : at + 64].astype(F32)
        grad = own[at : at + 64] + peer[at : at + 64].astype(F32)
        if at + 64 == length:
            grad = grad + jnp.concatenate([jnp.zeros((64 - HALO, width), F32), extra])
        scale = lax.rsqrt(jnp.mean(v * v, axis=-1, keepdims=True) + EPSILON)
        d = grad * gain[...]
        inner = jnp.sum(d * v, axis=-1, keepdims=True)
        out[at : at + 64] = (
            cot[at : at + 64].astype(F32)
            + scale * d
            - v * (scale * scale * scale / width * inner)
        )


def on_device(
    block_input,
    input_gain,
    gate_proj,
    x_proj,
    bc_proj,
    dt_proj,
    x_conv,
    bc_conv,
    dt_bias,
    a_log,
    skip_gain,
    gated_gain,
    out_proj,
    cotangent,
):
    length, width = block_input.shape[1:]
    shard, inner = gate_proj.shape
    heads = dt_proj.shape[1]
    size = inner // heads
    states = bc_proj.shape[1]
    half_bc = states // 2
    taps = x_conv.shape[0]
    both = inner + states
    full_inner = inner * lax.axis_size("tp")
    ctx, fsdp = lax.axis_size("ctx"), lax.axis_size("fsdp")
    place = jnp.stack([lax.axis_index(a) for a in ("fsdp", "ctx", "tp")]).astype(jnp.int32)
    rows, cot = block_input[0], cotangent[0]
    ext = HALO + length
    last_bit = bits_of("ctx")[-1]

    gain = input_gain[None]
    wide = both + LANES
    packed, edge_rows, dt_wide, halves = launch(
        pack_body,
        [
            ((shard // ctx, wide + 2 * inner), LOW),
            ((HALO, width), LOW),
            ((shard, LANES), LOW),
            ((2, length // 2, width), LOW),
        ],
        place,
        rows,
        cot,
        x_proj,
        bc_proj,
        dt_proj.T,
        gate_proj,
        out_proj,
        scratch=[((6 + inner // out_proj.shape[1],), None)],
        mib=58,
        hbm=(0, 1, 2, 3, 5, 6),
    )
    halves_far = far_halves(halves)
    halo = lax.ppermute(edge_rows, "ctx", [(i, i + 1) for i in range(ctx - 1)])
    [normed] = launch(norm_body, [((ext, width), LOW)], place, rows, halo, gain, mib=8)
    near = swap(packed, "fsdp", 1)
    [near] = launch(
        copy_body,
        [(packed.shape, LOW)],
        place,
        near,
        mib=4,
        deps=[normed, *halves_far.values()],
    )
    near_y = swap(near, "ctx", bits_of("ctx")[-1])
    found = {0: packed, 1: near}
    for bit in reversed(bits_of("fsdp")[1:]):
        for k in [k for k in found if k % 2 == 0]:
            found[k ^ bit] = swap(found[k], "fsdp", bit)
    for k in [k for k in found if k and k % 2 == 0]:
        [on] = launch(copy_body, [(packed.shape, LOW)], place, found[k], mib=4, deps=[near_y])
        found[k ^ 1] = swap(on, "fsdp", 1)
    far = [found[k] for k in range(1, fsdp)]
    by_distance = [spread(p, "ctx") for p in far]
    parts = [by_distance[k][j] for j in range(ctx) for k in range(fsdp - 1)]
    halves_all = across_tp(halves_far)

    bias_row, a_row, skip_row, gained = (
        dt_bias[None],
        a_log[None],
        skip_gain[None],
        gated_gain[None],
    )
    w_first, proj, conv_out, act, within, state, scalars, decay = launch(
        front_body(fsdp, ctx, taps, heads, size),
        [
            ((width, both + LANES), LOW),
            ((ext, both + LANES), F32),
            ((length, both), F32),
            ((length, both), F32),
            ((length, inner), F32),
            ((inner, half_bc), LOW),
            ((4, length, LANES), F32),
            ((8, LANES), F32),
        ],
        place,
        normed,
        x_proj,
        bc_proj,
        dt_wide,
        *parts,
        x_conv,
        bc_conv,
        bias_row,
        a_row,
        scratch=[((length, inner), LOW)],
    )
    other, kept, kept_decay = run_scan(place, state, decay, False, size, [halves_all[1]])
    gate_in, d_no, w_gate, w_out = launch(
        gate_body(fsdp, ctx),
        [
            ((length, inner), F32),
            ((length, inner), LOW),
            ((width, inner), LOW),
            ((inner, width), LOW),
        ],
        place,
        normed,
        cot,
        gate_proj,
        out_proj,
        *parts,
    )
    normed_seq, cot_seq = launch(
        sequence_body,
        [((HALO + ctx * length, width), LOW), ((ctx * length, width), LOW)],
        place,
        gain,
        rows,
        swap(rows, "ctx", 1),
        cot,
        swap(cot, "ctx", 1),
        *halves_all,
        scratch=[((ctx * length, width), LOW)],
        mib=4 + 10 * ctx // 4,
    )
    state_in, swept, sums = launch(
        mix_body(last_bit, size),
        [((inner, half_bc), LOW), ((length, inner), F32), ((8, length), F32)],
        place,
        other,
        kept,
        kept_decay,
        act,
        within,
        scalars,
        gate_in,
        d_no,
        skip_row,
        gained,
        deps=[normed_seq],
    )
    others = swap(sums, "tp", 1)
    w = inner // ctx
    normed_out, d_gate, d_mixed, d_scaled, state_grad, skip_rows, *sends = launch(
        turn_body(size, full_inner, ctx),
        [
            ((length, inner), LOW),
            ((length, inner), LOW),
            ((length, inner), F32),
            ((length, inner), LOW),
            ((inner, half_bc), LOW),
            ((8, inner), F32),
        ]
        + [((2, length, w), LOW)] * ctx,
        place,
        sums,
        others,
        act,
        swept,
        scalars,
        gate_in,
        d_no,
        skip_row,
        gained,
        scratch=[((ctx, 2, length, w), LOW)],
    )
    other, kept, kept_decay = run_scan(place, state_grad, decay, True, size)

    back, pair_t, half_out, branch = launch(
        local_body(heads, size),
        [
            ((length, inner), F32),
            ((length, length), F32),
            ((length, width), F32),
            ((length, width), LOW),
        ],
        place,
        d_mixed,
        act,
        scalars,
        rows,
        normed_out,
        w_out,
    )
    branch = swap(branch, "tp", 1)
    pieces = [sends[0]] + [swap(sends[k], "ctx", k) for k in range(1, ctx)]

    def partial_sums(count, columns, *args, stacked, deps=()):
        span = width // fsdp
        block = (fsdp // 2, count, columns, span)
        return launch(
            weights_body(fsdp, ctx, stacked),
            [(block, F32), (block, LOW)],
            place,
            *args,
            scratch=[((count, columns, width), F32)],
            mib=20,
            deps=deps,
        )

    def halve(keep, received, deps=()):
        block = (keep.shape[0] // 2, *keep.shape[1:])
        return launch(
            add_body, [(block, F32), (block, LOW)], place, keep, received, mib=10, deps=deps
        )

    pair_keep, pair_send = partial_sums(2, w, *pieces, normed_seq, cot_seq, stacked=True, deps=[other, back])
    pair_send_first = pair_send
    fsdp_bits = bits_of("fsdp")
    received = swap(pair_send, "fsdp", 1)
    for bit in fsdp_bits[1:]:
        pair_keep, pair_send = halve(pair_keep, received)
        received = swap(pair_send, "fsdp", bit)
    r = 4 * LANES // ctx
    d_first, small, *first_sends = launch(
        rear_body(last_bit, ctx, taps, heads, size),
        [((ext, both + LANES), LOW), ((8, inner), F32)] + [((ext, w + r), LOW)] * ctx,
        place,
        other,
        kept,
        kept_decay,
        back,
        pair_t,
        act,
        conv_out,
        proj,
        scalars,
        swept,
        d_mixed,
        d_scaled,
        state_in,
        skip_row,
        skip_rows,
        x_conv,
        bc_conv,
        bias_row,
        a_row,
        scratch=[
            ((ext + HALO, both), F32),
            ((length, inner), LOW),
            ((length, inner), F32),
            ((length, inner), F32),
            ((ctx, ext, w + r), LOW),
        ],
        deps=[pair_send_first],
    )
    first_pieces = [first_sends[0]] + [swap(first_sends[k], "ctx", k) for k in range(1, ctx)]
    own_grad, send_grad, edge, tally = launch(
        down_body,
        [((length, width), F32), ((length, width), LOW), ((HALO, width), LOW), ((8, width), F32)],
        place,
        d_first,
        d_gate,
        w_first,
        w_gate,
        rows,
        halo,
        small,
        deps=[pair_send, branch],
    )

    def add_tally(tally, axis, bit):
        return launch(
            tally_body(axis == "tp"),
            [(tally.shape, F32)],
            place,
            tally,
            swap(tally, axis, bit),
            mib=2,
        )[0]

    high, fsdp_high = bits_of("ctx")[1:], bits_of("fsdp")[1:]
    for hop in [("ctx", b) for b in high[:-1]] + [("fsdp", b) for b in fsdp_high[:-1]]:
        tally = add_tally(tally, *hop)
    [pair_own] = launch(
        last_add_body, [((2, w, width // fsdp), LOW)], place, pair_keep, received, mib=10
    )
    tally, keep, send = launch(
        with_tally(weights_body(fsdp, ctx, False), ctx + 1),
        [
            (tally.shape, F32),
            ((fsdp // 2, 1, w + r, width // fsdp), F32),
            ((fsdp // 2, 1, w + r, width // fsdp), LOW),
        ],
        place,
        tally,
        swap(tally, "ctx", 1),
        *first_pieces,
        normed_seq,
        scratch=[((1, w + r, width), F32)],
        mib=20,
    )
    back_one = [(i + 1, i) for i in range(ctx - 1)]
    edge_in = lax.ppermute(edge, "ctx", back_one)
    edge_peer = swap(edge_in, "tp", 1)
    received = swap(send, "fsdp", 1)
    tally = add_tally(tally, "ctx", high[-1])
    tally_in = swap(tally, "tp", 1)
    [block_output] = launch(
        output_body, [((length, width), LOW)], place, half_out, branch, mib=8
    )
    [input_grad] = launch(
        finish_body,
        [((length, width), F32)],
        place,
        own_grad,
        swap(send_grad, "tp", 1),
        edge_in,
        edge_peer,
        rows,
        cot,
        gain,
        mib=24,
    )
    block = (keep.shape[0] // 2, *keep.shape[1:])
    tally, keep, send = launch(
        with_tally(add_body, 2, True),
        [(tally.shape, F32), (block, F32), (block, LOW)],
        place,
        tally,
        tally_in,
        keep,
        received,
        mib=10,
        deps=[input_grad, block_output],
    )
    received = swap(send, "fsdp", fsdp_bits[1])
    for bit in fsdp_bits[2:]:
        keep, send = halve(keep, received)
        received = swap(send, "fsdp", bit)
    pair_all = [pair_own] + [swap(pair_own, "ctx", k) for k in range(1, ctx)]
    tally, first_own, last_own = launch(
        with_tally(last_add_body, 2),
        [
            (tally.shape, F32),
            ((1, w, width // fsdp), LOW),
            ((1, r, width // fsdp), LOW),
        ],
        place,
        tally,
        swap(tally, "fsdp", 1),
        keep,
        received,
        mib=10,
    )
    first_all = spread(first_own, "ctx")
    [last_own] = launch(
        join_body(states),
        [(last_own.shape, LOW)],
        place,
        last_own,
        swap(last_own, "tp", 1),
        mib=2,
        deps=[first_all[2]],
    )
    last_all = spread(last_own, "ctx")
    grad_gate, grad_out = launch(
        close_pair_body(ctx),
        [((shard, inner), F32), ((inner, out_proj.shape[1]), F32)],
        place,
        *pair_all,
        scratch=[((ctx, w, shard), F32)],
        mib=12,
        deps=[last_all[2]],
    )
    pair_outs = [((shard, inner), F32), ((inner, out_proj.shape[1]), F32)]
    first_outs = [((shard, inner), F32), ((shard, states), F32), ((heads, shard), F32)]
    small_outs = [((1, width), F32), ((taps, states), F32), ((taps, inner), F32), ((1, inner), F32)]
    small_outs += [((1, heads), F32)] * 3
    grad_gate, grad_out, grad_x, grad_bc, grad_dt, *smalls = launch(
        end_body(ctx, states, heads),
        pair_outs + first_outs + small_outs,
        place,
        *pair_all,
        *first_all,
        *last_all,
        tally,
        swap(tally, "fsdp", fsdp_high[-1]),
        scratch=[
            ((ctx, w, shard), F32),
            ((ctx, w, shard), F32),
            ((r * ctx, shard), F32),
        ],
        mib=24,
    )
    grad_gain, bc_taps, x_taps, grad_gated, grad_bias, grad_a, grad_skip = smalls
    return (
        block_output[None],
        input_grad[None],
        grad_gain[0],
        grad_gate,
        grad_x,
        grad_bc,
        grad_dt.T,
        x_taps,
        bc_taps,
        grad_bias[0],
        grad_a[0],
        grad_skip[0],
        grad_gated[0],
        grad_out,
    )


def solution(mesh):
    rows = P("fsdp", "ctx", None)
    both = P("fsdp", "tp")
    head = P("tp")
    in_specs = (
        rows,
        P(),
        both,
        both,
        P("fsdp", None),
        both,
        P(None, "tp"),
        P(),
        head,
        head,
        head,
        head,
        P("tp", "fsdp"),
        rows,
    )
    out_specs = (
        rows,
        rows,
        P(),
        both,
        both,
        P("fsdp", None),
        both,
        P(None, "tp"),
        P(),
        head,
        head,
        head,
        head,
        P("tp", "fsdp"),
    )
    return jax.shard_map(
        on_device, mesh=mesh, in_specs=in_specs, out_specs=out_specs, check_vma=False
    )
```
